256 devices in a mesh: lat: 16 (over z_lo, y, core), lev: 4 (over x), ocn: 4 (over z_hi).
Axes of the slice: x: 4, y: 4, z: 8 (z_hi: 4, z_lo: 2; z = z_hi * 2 + z_lo), core: 2. Of those that a mesh axis runs over, the one named last changes fastest.
Arguments:
- atmos_fields: bfloat16 [2, 24, 2560, 5632], P(None, 'lev', ('lat', 'ocn')), may hold values from -6 to 6
- lat_points: int32 [2560], P(('lat', 'ocn')), may hold values from 20 to 5632, as said below
- wave_order: int32 [256], replicated, may hold values from 0 to 255, each once
- legendre: bfloat16 [256, 2560, 1536], P(('lat', 'ocn'), None, 'lev'), may hold values from -0.125 to 0.125
- column_weight: bfloat16 [2, 24], P(None, 'lev'), may hold values from -1.25 to 1.25
- block_remap: int32 [2560, 44], P(('lat', 'ocn'), 'lev'), may hold values from 0 to 17407, as said below
- ocean_temp: float32 [1024, 2176], P(('lat', 'ocn')), may hold values from -6 to 6
- ocean_salt: float32 [1024, 2176], P(('lat', 'ocn')), may hold values from -6 to 6
- sea_mask: int32 [1024, 17], P(('lat', 'ocn')), may hold values 0 or 1
Outputs:
- spectra: float32 [256, 96, 1536], P(('lat', 'ocn'), None, 'lev')
- temp_next: float32 [1024, 2176], P(('lat', 'ocn'))
- salt_next: float32 [1024, 2176], P(('lat', 'ocn'))
- surface_temp: float32 [2560, 5632], P(('lat', 'ocn'), 'lev')
The draws below stay inside these ranges and needn't reach their ends.
Inputs may be any that keep to these rules, and one draw needn't show every extreme that they name: `lat_points`: a multiple of 4 for every latitude row. `wave_order`: each wavenumber appears once. `block_remap`: the blocks of latitude band g (rows g * 40 onward) name tiles of ocean sections g - 1, g or g + 1 only; section g holds tiles g * 16 * 17 onward, in row order.
All inputs are finite; a program needn't handle non-finite values. No bound on the sum of `sea_mask` on one device may be relied on, other than what follows from the above.
Results may differ from the reference program's by a relative error of at most 0.0037.
Values may be sent and summed in bfloat16 or wider, within the bound.
A program may use at most 128 MiB of HBM per device.

```python
import math
import jax
import jax.numpy as jnp
from jax import lax

FIELDS = 2
LEVELS = 24
BANDS = 64
NLAT = 2560
NLON = 5632
BLOCK = 128
WAVES = 256
DEGREES = 1536
OROW_DEV = 16
OCOLS = 2176
OROWS = 1024
TILES = 17408


def draw_lat_points(key, part):
    row_index = jnp.arange(NLAT, dtype=jnp.int32)
    jitter = jax.random.randint(key, (NLAT,), 0, 8)
    jitter = jitter.at[0].set(0)
    return jnp.minimum(NLON, 20 + 4 * row_index + 4 * jitter).astype(jnp.int32)


def draw_block_remap(key, part):
    blocks_row = NLON // BLOCK
    per_band = NLAT // BANDS
    tile_count = OROW_DEV * OCOLS // BLOCK
    band_of = (jnp.arange(NLAT, dtype=jnp.int32) // per_band)[:, None]
    key_step = jax.random.fold_in(key, 11)
    key_tile = jax.random.fold_in(key, 23)
    offset = jax.random.randint(key_step, (NLAT, blocks_row), -1, 2)
    target = jnp.clip(band_of + offset, 0, BANDS - 1)
    within = jax.random.randint(key_tile, (NLAT, blocks_row), 0, tile_count)
    result = target * tile_count + within
    result = result.at[0, 0].set(0)
    result = result.at[NLAT - 1, blocks_row - 1].set(BANDS * tile_count - 1)
    return result.astype(jnp.int32)


def plant(values, key, least, top_value):
    longest = values.shape.index(max(values.shape))
    spots = []
    for shift in (0, 1):
        where = [jax.random.randint(jax.random.fold_in(key, axis), (), 0, length) for axis, length in enumerate(values.shape)]
        where[longest] = (where[longest] + shift) % values.shape[longest]
        spots.append(tuple(where))
    return values.at[spots[0]].set(least).at[spots[1]].set(top_value)


def level_of(key, shape, pieces, least, top_value):
    def one(dim, blocks):
        heights = jax.random.uniform(jax.random.fold_in(jax.random.fold_in(key, 6), dim), (blocks,), jnp.float32, least / len(pieces), top_value / len(pieces))
        return jnp.repeat(jnp.exp(heights), shape[dim] // blocks).reshape((-1,) + (1,) * (len(shape) - dim - 1))

    loudness = one(*pieces[0])
    for cut in pieces[1:]:
        loudness = loudness * one(*cut)
    return loudness


def noise(rng, extent, deviation, reach, shards=(), kind=jnp.bfloat16):
    values = jax.random.normal(rng, extent, jnp.float32) * deviation
    if len(shards) > 0:
        values = level_of(rng, extent, shards, -0.22, 0.18) * values
    return jnp.clip(values, min=-reach, max=reach).astype(kind)


def setup_inputs(seed: int = 0) -> dict:
    seeds = jax.random.split(jax.random.key(seed), 10)
    return {
        "atmos_fields": noise(seeds[0], (FIELDS, LEVELS, NLAT, NLON), 1.0, 6.0, ((1, 4), (2, 64))),
        "lat_points": draw_lat_points(jax.random.fold_in(seeds[9], 71), 0),
        "wave_order": jax.random.permutation(seeds[2], WAVES).astype(jnp.int32),
        "legendre": noise(seeds[3], (WAVES, NLAT, DEGREES), NLAT ** -0.5, 0.125, ((0, 64), (2, 4))),
        "column_weight": noise(seeds[4], (FIELDS, LEVELS), LEVELS ** -0.5, 1.25, ((1, 4),)),
        "block_remap": draw_block_remap(jax.random.fold_in(seeds[9], 71), 0),
        "ocean_temp": noise(seeds[6], (OROWS, OCOLS), 1.0, 6.0, ((0, 64),), jnp.float32),
        "ocean_salt": noise(seeds[7], (OROWS, OCOLS), 1.0, 6.0, ((0, 64),), jnp.float32),
        "sea_mask": plant((jax.random.randint(seeds[8], (OROWS, OCOLS // BLOCK), 0, 4) < 3).astype(jnp.int32), jax.random.fold_in(seeds[8], 1), 0, 1),
    }


FULL_TURN = 2.0 * math.pi
DIFFUSION = 0.2
COUPLING = 0.5

def fourier_table(wave_order, length):
    points = jnp.arange(length, dtype=jnp.int32)
    phase = wave_order[None, :] * points[:, None] % length
    angle = phase.astype(jnp.float32) * (FULL_TURN / length)
    table = jnp.concatenate([jnp.cos(angle), -jnp.sin(angle)], axis=1).astype(jnp.bfloat16)
    return (table, points)

def reference(atmos_fields, lat_points, wave_order, legendre, column_weight, block_remap, ocean_temp, ocean_salt, sea_mask):
    table, points = fourier_table(wave_order, NLON)
    point_mask = points[None, :] < lat_points[:, None]
    masked = jnp.where(point_mask[None, None], atmos_fields, jnp.zeros((), jnp.bfloat16))
    raw_sums = jnp.dot(masked.reshape(-1, NLON), table, preferred_element_type=jnp.float32)
    raw_sums = raw_sums.reshape(FIELDS, LEVELS, NLAT, 2, WAVES)
    inverse_root = 1.0 / jnp.sqrt(lat_points.astype(jnp.float32))
    weights = jnp.where(2 * wave_order[None, :] < lat_points[:, None], inverse_root[:, None], jnp.zeros((), jnp.float32))
    coeffs = (raw_sums * weights[None, None, :, None, :]).astype(jnp.bfloat16)
    coeffs = coeffs.transpose(4, 1, 0, 3, 2).reshape(WAVES, LEVELS * FIELDS * 2, NLAT)
    spectra = lax.map(lambda slot_pair: jnp.dot(slot_pair[0], slot_pair[1], preferred_element_type=jnp.float32), (coeffs, legendre))
    columns = jnp.stack([jnp.dot(column_weight[field_idx], masked[field_idx].reshape(LEVELS, -1), preferred_element_type=jnp.float32) for field_idx in range(FIELDS)])
    blocks = columns.reshape(FIELDS, NLAT, NLON // BLOCK, BLOCK).transpose(1, 2, 0, 3).reshape(-1, FIELDS * BLOCK)
    tile_sums = jax.ops.segment_sum(blocks, block_remap.reshape(-1), num_segments=TILES)
    forcing = tile_sums.reshape(OROWS, OCOLS // BLOCK, FIELDS, BLOCK).transpose(2, 0, 1, 3).reshape(FIELDS, OROWS, OCOLS)
    sea_cells = jnp.broadcast_to(sea_mask[:, :, None], (OROWS, OCOLS // BLOCK, BLOCK)).reshape(OROWS, OCOLS).astype(jnp.float32)
    ocean_state = jnp.stack([ocean_temp, ocean_salt])
    padded = jnp.pad(ocean_state, ((0, 0), (1, 1), (0, 0)))
    laplace = padded[:, 2:] + padded[:, :-2] + jnp.roll(ocean_state, 1, 2) + jnp.roll(ocean_state, -1, 2) - 4.0 * ocean_state
    updated = ocean_state + DIFFUSION * laplace + COUPLING * sea_cells[None] * forcing
    temp_next = updated[0]
    salt_next = updated[1]
    surface = temp_next.reshape(TILES, BLOCK)[block_remap.reshape(-1)].reshape(NLAT, NLON)
    surface_temp = jnp.where(point_mask, surface, jnp.zeros((), jnp.float32))
    return (spectra, temp_next, salt_next, surface_temp)
```

```python
import math

import jax
import jax.numpy as jnp
from jax import lax
from jax.experimental import pallas as pl
from jax.experimental.pallas import tpu as pltpu
from jax.sharding import PartitionSpec as P

BLOCK = 128
FULL_TURN = 2.0 * math.pi
DIFFUSION = 0.2
COUPLING = 0.5
CHUNK = 512


def local_kernel(
    x_ref, lat_ref, wcol_ref, root_ref, slot_ref, fine1_ref, fine2_ref, coarse1_ref, coarse2_ref,
    msg_ref, tiles_ref, masked, table, acc, blocks_hi, blocks_lo,
):
    step = pl.program_id(0)
    pair_rows = lat_ref.shape[0]
    pairs = x_ref.shape[0] // pair_rows
    band = pair_rows // 2
    width = x_ref.shape[1]
    blocks = width // BLOCK

    for a in range(blocks):
        row1 = coarse1_ref[0, a : a + 1, :]
        row2 = coarse2_ref[0, a : a + 1, :]
        table[a * BLOCK : (a + 1) * BLOCK, :] = (
            fine1_ref[...] * row1 + fine2_ref[...] * row2
        ).astype(jnp.bfloat16)

    points = step * width + lax.broadcasted_iota(jnp.int32, (pair_rows, width), 1)
    keep = points < lat_ref[...]
    for f in range(2):
        total = None
        for p in range(pairs // 2):
            rows = slice((f * (pairs // 2) + p) * pair_rows, (f * (pairs // 2) + p + 1) * pair_rows)
            part = jnp.where(keep, x_ref[rows, :].astype(jnp.float32), 0.0)
            masked[rows, :] = part.astype(jnp.bfloat16)
            term = part * wcol_ref[rows, :]
            total = term if total is None else total + term
        flux = total[:band] + total[band:]
        for two in range(blocks // 2):
            pair = jnp.concatenate(
                [flux[:, (2 * two) * BLOCK : (2 * two + 1) * BLOCK], flux[:, (2 * two + 1) * BLOCK : (2 * two + 2) * BLOCK]],
                axis=0,
            )
            high = pair.astype(jnp.bfloat16)
            low = (pair - high.astype(jnp.float32)).astype(jnp.bfloat16)
            start = pl.multiple_of((step * (blocks // 2) + two) * pair_rows, 16)
            blocks_hi[pl.ds(start, pair_rows), f * BLOCK : (f + 1) * BLOCK] = high
            blocks_lo[pl.ds(start, pair_rows), f * BLOCK : (f + 1) * BLOCK] = low

    rows = x_ref.shape[0]
    product = jnp.dot(masked[...], table[...], preferred_element_type=jnp.float32)

    @pl.when(step == 0)
    def _():
        acc[:rows, :] = product
        acc[rows:, :] = jnp.zeros((acc.shape[0] - rows, acc.shape[1]), jnp.float32)

    @pl.when(step > 0)
    def _():
        acc[:rows, :] += product

    @pl.when(step == pl.num_programs(0) - 1)
    def _():
        for p in range(pairs):
            acc[p * pair_rows : (p + 1) * pair_rows, :] *= root_ref[...]
        turned = acc[...].T.astype(jnp.bfloat16)
        msg_ref[...] = turned.reshape(msg_ref.shape)
        part_rows = tiles_ref.shape[2]
        for sec in range(3):
            for h in range(2):
                base = (sec * 2 + h) * part_rows
                ids = base + lax.broadcasted_iota(jnp.int32, (part_rows, slot_ref.shape[1]), 0)
                hot = jnp.where(slot_ref[...] == ids, 1.0, 0.0).astype(jnp.bfloat16)
                sums = jnp.dot(hot, blocks_hi[...], preferred_element_type=jnp.float32)
                sums += jnp.dot(hot, blocks_lo[...], preferred_element_type=jnp.float32)
                for f in range(2):
                    tiles_ref[sec, f * 2 + h] = sums[:, f * BLOCK : (f + 1) * BLOCK].astype(tiles_ref.dtype)


def local_part(fields, lat_points, wave_order, column_weight, slots, groups):
    nf, nl, band, length = fields.shape
    rows = nf * nl * band
    waves = wave_order.shape[0]
    each = waves // groups
    cols = 2 * waves
    order = jnp.broadcast_to(wave_order.reshape(groups, 1, each), (groups, 2, each)).reshape(1, cols)
    imag = (lax.broadcasted_iota(jnp.int32, (1, cols), 1) // each) % 2 == 1
    unit = FULL_TURN / length
    fine = (order * jnp.arange(BLOCK, dtype=jnp.int32)[:, None] % length).astype(jnp.float32) * unit
    coarse = (
        order * (BLOCK * jnp.arange(length // BLOCK, dtype=jnp.int32)[:, None]) % length
    ).astype(jnp.float32) * unit
    fc, fs = jnp.cos(fine), jnp.sin(fine)
    cc, cs = jnp.cos(coarse), jnp.sin(coarse)
    fine1, fine2 = jnp.where(imag, fs, fc), jnp.where(imag, fc, fs)
    coarse1, coarse2 = jnp.where(imag, -cc, cc), -cs
    steps = length // CHUNK
    coarse1 = coarse1.reshape(steps, CHUNK // BLOCK, cols)
    coarse2 = coarse2.reshape(steps, CHUNK // BLOCK, cols)
    inverse_root = 1.0 / jnp.sqrt(lat_points.astype(jnp.float32))
    root = jnp.where(2 * order < lat_points[:, None], inverse_root[:, None], 0.0)
    root = jnp.concatenate([root, root], axis=0)
    lat2 = jnp.concatenate([lat_points, lat_points])[:, None]
    wcol = jnp.broadcast_to(column_weight.astype(jnp.float32)[:, :, None], (nf, nl, band)).reshape(rows, 1)
    slot_row = slots.T.reshape(1, -1)
    whole = lambda shape: pl.BlockSpec(shape, lambda i: (0,) * len(shape))
    lanes = 512
    tile_parts = (3, 4, 136, BLOCK)
    return pl.pallas_call(
        local_kernel,
        grid=(steps,),
        in_specs=[
            pl.BlockSpec((rows, CHUNK), lambda i: (0, i)),
            whole(lat2.shape),
            whole(wcol.shape),
            whole(root.shape),
            whole(slot_row.shape),
            whole(fine1.shape),
            whole(fine2.shape),
            pl.BlockSpec((1, CHUNK // BLOCK, cols), lambda i: (i, 0, 0)),
            pl.BlockSpec((1, CHUNK // BLOCK, cols), lambda i: (i, 0, 0)),
        ],
        out_specs=[whole((groups, 2 * each, lanes)), whole(tile_parts)],
        out_shape=[
            jax.ShapeDtypeStruct((groups, 2 * each, lanes), jnp.bfloat16),
            jax.ShapeDtypeStruct(tile_parts, jnp.float32),
        ],
        scratch_shapes=[
            pltpu.VMEM((rows, CHUNK), jnp.bfloat16),
            pltpu.VMEM((CHUNK, cols), jnp.bfloat16),
            pltpu.VMEM((lanes, cols), jnp.float32),
            pltpu.VMEM((slot_row.shape[1], 2 * BLOCK), jnp.bfloat16),
            pltpu.VMEM((slot_row.shape[1], 2 * BLOCK), jnp.bfloat16),
        ],
        compiler_params=pltpu.CompilerParams(vmem_limit_bytes=48 * 1024 * 1024),
    )(fields.reshape(rows, length), lat2, wcol, root, slot_row, fine1, fine2, coarse1, coarse2)


def ring_gather(piece, axis):
    count = lax.axis_size(axis)
    me = lax.axis_index(axis)
    pieces = [piece]
    for hop in range(1, count):
        pieces.append(lax.ppermute(piece, axis, [(i, (i + hop) % count) for i in range(count)]))
    twice = jnp.stack(pieces[::-1] + pieces[::-1])
    return lax.dynamic_slice_in_dim(twice, count - 1 - me, count, 0)


def body(
    atmos_fields,
    lat_points,
    wave_order,
    legendre,
    column_weight,
    block_remap,
    ocean_temp,
    ocean_salt,
    sea_mask,
):
    both = ("lat", "ocn")
    nf, nl, band, length = atmos_fields.shape
    groups = lax.axis_size(both)
    levs = lax.axis_size("lev")
    g = lax.axis_index(both)
    orow, ocols = ocean_temp.shape
    tcols = ocols // BLOCK
    tile_count = orow * tcols

    def slot_of(targets):
        local = targets - (g - 1) * tile_count
        sec, inside = local // tile_count, local % tile_count
        r, c = inside // tcols, inside % tcols
        return sec * tile_count + (r // 8) * (tcols * 8) + c * 8 + r % 8

    remap = ring_gather(block_remap, "lev").transpose(1, 0, 2).reshape(band, -1)
    msg, parts = local_part(
        atmos_fields, lat_points, wave_order, column_weight, slot_of(remap), groups
    )
    got = lax.all_to_all(msg, both, split_axis=0, concat_axis=0, tiled=True)
    each = wave_order.shape[0] // groups
    own = got[:, :, : nf * nl * band].reshape(groups, 2, each, nf, nl, band)
    own = own.transpose(2, 4, 3, 1, 0, 5).reshape(each, nl * nf * 2, groups * band)
    coeffs = ring_gather(own, "lev").transpose(1, 0, 2, 3).reshape(each, levs * nl * nf * 2, groups * band)
    spectra = jnp.einsum("srj,sjd->srd", coeffs, legendre, preferred_element_type=jnp.float32)

    up = [(i, (i + 1) % groups) for i in range(groups)]
    down = [((i + 1) % groups, i) for i in range(groups)]
    arrived = parts[1] + lax.ppermute(parts[2], both, up) + lax.ppermute(parts[0], both, down)
    sums = jnp.sum(lax.all_to_all(arrived, "lev", split_axis=0, concat_axis=0, tiled=True).reshape(levs, -1, BLOCK), 0)
    sums = ring_gather(sums, "lev")
    forcing = (
        sums.reshape(2, orow // 8, tcols, 8, BLOCK).transpose(0, 1, 3, 2, 4).reshape(2, orow, ocols)
    )
    sea = jnp.broadcast_to(sea_mask[:, :, None], (orow, tcols, BLOCK)).reshape(orow, ocols).astype(jnp.float32)
    state = jnp.stack([ocean_temp, ocean_salt])
    above = lax.ppermute(state[:, -1:], both, up[:-1])
    below = lax.ppermute(state[:, :1], both, down[:-1])
    padded = jnp.concatenate([above, state, below], axis=1)
    laplace = (
        padded[:, 2:] + padded[:, :-2] + jnp.roll(state, 1, 2) + jnp.roll(state, -1, 2) - 4.0 * state
    )
    updated = state + DIFFUSION * laplace + COUPLING * sea[None] * forcing
    temp_next, salt_next = updated[0], updated[1]
    near = jnp.concatenate(
        [lax.ppermute(temp_next, both, up), temp_next, lax.ppermute(temp_next, both, down)], axis=0
    ).reshape(3 * tile_count, BLOCK)
    local = block_remap.reshape(-1) - (g - 1) * tile_count
    quarter = length // levs
    surface = jnp.take(near, local, axis=0).reshape(band, quarter)
    own_points = lax.axis_index("lev") * quarter + jnp.arange(quarter, dtype=jnp.int32)
    surface_temp = jnp.where(own_points[None, :] < lat_points[:, None], surface, 0.0)
    return (spectra, temp_next, salt_next, surface_temp)


def solution(mesh):
    both = ("lat", "ocn")
    placed = (
        P(None, "lev", both, None),
        P(both),
        P(),
        P(both, None, "lev"),
        P(None, "lev"),
        P(both, "lev"),
        P(both, None),
        P(both, None),
        P(both, None),
    )
    return jax.shard_map(
        body,
        mesh=mesh,
        in_specs=placed,
        out_specs=(P(both, None, "lev"), P(both, None), P(both, None), P(both, "lev")),
        check_vma=False,
    )
```

```python
import functools
import math

import jax
import jax.numpy as jnp
import numpy as np
from jax import lax
from jax.experimental import pallas as pl
from jax.experimental.pallas import tpu as pltpu
from jax.sharding import PartitionSpec as P

BLOCK = 128
FULL_TURN = 2.0 * math.pi
DIFFUSION = 0.2
COUPLING = 0.5
CHUNK = 512
MESH = pl.DeviceIdType.MESH
F32 = jnp.float32
BF16 = jnp.bfloat16


def cos_sin(phase, length):
    quarter = length // 4
    turns = sum((phase >= quarter // 2 + i * quarter).astype(jnp.int32) for i in range(4))
    t = (phase - turns * quarter).astype(F32) * (FULL_TURN / length)
    u = t * t
    c = 1.0 + u * (-1 / 2 + u * (1 / 24 + u * (-1 / 720 + u * (1 / 40320 - u / 3628800))))
    s = t * (1.0 + u * (-1 / 6 + u * (1 / 120 + u * (-1 / 5040 + u * (1 / 362880)))))
    odd = (turns == 1) | (turns == 3)
    cos = jnp.where(odd, s, c)
    sin = jnp.where(odd, c, s)
    cos = jnp.where((turns == 1) | (turns == 2), -cos, cos)
    sin = jnp.where((turns == 2) | (turns == 3), -sin, sin)
    return cos, sin


def modulo(value, length):
    whole = jnp.floor((value.astype(F32) + 0.5) * (1.0 / length)).astype(jnp.int32)
    return value - whole * length


def local_kernel(
    lat_ref, weight_ref, x_ref, wave_ref,
    msg_ref, high_ref, low_ref,
    masked, table, acc, padded, blocks, fine, coarse, lat_col,
):
    step = pl.program_id(0)
    rows, width = x_ref.shape
    waves = wave_ref.shape[1]
    band = lat_ref.shape[0]
    pair_rows = 2 * band
    pairs = rows // pair_rows
    parts = width // BLOCK
    steps = pl.num_programs(0)
    coarse_count = coarse.shape[1]
    length = coarse_count * BLOCK
    quarter = blocks.shape[0] // 4
    quarter_blocks = coarse_count // 4

    @pl.when(step == 0)
    def _():
        wave = wave_ref[...]
        offsets = lax.broadcasted_iota(jnp.int32, (BLOCK, waves), 0)
        fine[0], fine[1] = cos_sin(modulo(offsets * wave, length), length)
        starts = lax.broadcasted_iota(jnp.int32, (coarse_count, waves), 0)
        coarse[0], coarse[1] = cos_sin(BLOCK * modulo(starts * wave, coarse_count), length)
        for j in range(band):
            row = jnp.full((1, BLOCK), lat_ref[j], jnp.int32)
            lat_col[j : j + 1, :] = row
            lat_col[band + j : band + j + 1, :] = row
        for q in range(4):
            blocks[q * quarter + quarter_blocks * band : (q + 1) * quarter, :] = jnp.zeros(
                (quarter - quarter_blocks * band, 2 * BLOCK), F32
            )

    fc, fs = fine[0], fine[1]
    for a in range(parts):
        at = step * parts + a
        cc = coarse[0, pl.ds(at, 1), :]
        cs = coarse[1, pl.ds(at, 1), :]
        table[a * BLOCK : (a + 1) * BLOCK, :waves] = (fc * cc - fs * cs).astype(BF16)
        table[a * BLOCK : (a + 1) * BLOCK, waves:] = (-(fs * cc) - fc * cs).astype(BF16)

    lanes = lax.broadcasted_iota(jnp.int32, (pair_rows, BLOCK), 1)
    upper = lax.broadcasted_iota(jnp.int32, (pair_rows, BLOCK), 0) < band
    levels = rows // (2 * band)
    for a in range(parts):
        cols = slice(a * BLOCK, (a + 1) * BLOCK)
        keep = lanes + (step * width + a * BLOCK) < lat_col[...]
        at = step * parts + a
        start = pl.multiple_of((at // quarter_blocks) * quarter + (at % quarter_blocks) * band, 8)
        for f in range(2):
            total = None
            for p in range(pairs // 2):
                here = slice((f * (pairs // 2) + p) * pair_rows, (f * (pairs // 2) + p + 1) * pair_rows)
                part = jnp.where(keep, x_ref[here, cols].astype(F32), 0.0)
                masked[here, cols] = part.astype(BF16)
                scale = jnp.where(
                    upper, weight_ref[f * levels + 2 * p], weight_ref[f * levels + 2 * p + 1]
                )
                term = part * scale
                total = term if total is None else total + term
            blocks[pl.ds(start, band), f * BLOCK : (f + 1) * BLOCK] = total[:band] + total[band:]

    product = jnp.dot(masked[...], table[...], preferred_element_type=F32)

    @pl.when(step == 0)
    def _():
        acc[...] = product

    @pl.when(step > 0)
    def _():
        acc[...] += product

    @pl.when(step == steps - 1)
    def _():
        group = 3 * band
        lat = lat_col[:band, :]
        root = 1.0 / jnp.sqrt(lat.astype(F32))
        for n in range(waves // BLOCK):
            wave = wave_ref[:, n * BLOCK : (n + 1) * BLOCK]
            weight = jnp.where(2 * wave < lat, root, 0.0)
            for c in range(2):
                cols = slice(c * waves + n * BLOCK, c * waves + (n + 1) * BLOCK)
                for fl in range(rows // band):
                    base = (fl // 3) * BLOCK + (fl % 3) * band
                    padded[base : base + band, cols] = acc[fl * band : (fl + 1) * band, cols] * weight
        for t in range(rows // group):
            padded[t * BLOCK + group : (t + 1) * BLOCK, :] = jnp.zeros((BLOCK - group, 2 * waves), F32)
        turned = padded[...].T
        total_lanes = turned.shape[1]
        real = turned[:waves].reshape(waves // 8, 8, total_lanes)
        imag = turned[waves:].reshape(waves // 8, 8, total_lanes)
        first = lax.broadcasted_iota(jnp.int32, real.shape, 1) < 4
        even = jnp.where(first, real, pltpu.roll(imag, 4, 1))
        odd = jnp.where(first, pltpu.roll(real, 4, 1), imag)
        both = jnp.stack([even, odd], axis=1).reshape(msg_ref.shape)
        msg_ref[...] = both.astype(BF16)
        high = blocks[...].astype(BF16)
        high_ref[...] = high
        low_ref[...] = (blocks[...] - high.astype(F32)).astype(BF16)


def local_part(fields, lat_points, wave_order, column_weight):
    nf, nl, band, length = fields.shape
    rows = nf * nl * band
    waves = wave_order.shape[0]
    whole = lambda shape: pl.BlockSpec(shape, lambda i, *_: (0,) * len(shape))
    lanes = rows // (3 * band) * BLOCK
    count = length // BLOCK
    outs = [((waves // 4, 8, lanes), BF16), ((2048, 2 * BLOCK), BF16), ((2048, 2 * BLOCK), BF16)]
    return pl.pallas_call(
        local_kernel,
        grid_spec=pltpu.PrefetchScalarGridSpec(
            num_scalar_prefetch=2,
            grid=(length // CHUNK,),
            in_specs=[pl.BlockSpec((rows, CHUNK), lambda i, *_: (0, i)), whole((1, waves))],
            out_specs=[whole(shape) for shape, _ in outs],
            scratch_shapes=[
                pltpu.VMEM((rows, CHUNK), BF16),
                pltpu.VMEM((CHUNK, 2 * waves), BF16),
                pltpu.VMEM((rows, 2 * waves), F32),
                pltpu.VMEM((lanes, 2 * waves), F32),
                pltpu.VMEM((2048, 2 * BLOCK), F32),
                pltpu.VMEM((2, BLOCK, waves), F32),
                pltpu.VMEM((2, count, waves), F32),
                pltpu.VMEM((2 * band, BLOCK), jnp.int32),
            ],
        ),
        out_shape=[jax.ShapeDtypeStruct(*o) for o in outs],
        compiler_params=pltpu.CompilerParams(vmem_limit_bytes=32 * 1024 * 1024),
    )(
        lat_points,
        column_weight.astype(F32).reshape(-1),
        fields.reshape(rows, length),
        wave_order.reshape(1, waves),
    )


def link_kernel(
    sizes,
    lat_ref, msg_ref, high_ref, low_ref, slot_ref, temp_ref, salt_ref, sea_ref, want_ref, leg_hbm,
    spectra_ref, temp_out, salt_out, surface_ref,
    leg, arrived, gathered, regroup, parts, sums, slots, edge_from, edge_to, fresh, fresh_half, near, near_half,
    leg_sem, a2a_send, a2a_recv, slot_send, slot_recv, edge_send, edge_recv, part_send, part_recv,
    ring_send, left_recv, right_recv, far_recv, out_send, out_recv, half_send, half_recv, own_sem,
):
    nlat, nlev, nocn = sizes
    groups = nlat * nocn
    lat_at, q, ocn_at = lax.axis_index("lat"), lax.axis_index("lev"), lax.axis_index("ocn")
    g = lat_at * nocn + ocn_at
    section = groups // 4
    high_at, low_at = g // section, g % section
    band = lat_ref.shape[0]

    def device(group, lev):
        return (group // nocn, lev, group % nocn)

    def beside(offset):
        return (g + groups + offset) % groups

    def other(k):
        return (q + k) % nlev

    leg_copy = pltpu.make_async_copy(leg_hbm, leg, leg_sem)
    leg_copy.start()

    barrier = pltpu.get_barrier_semaphore()

    def greet(k, _):
        pl.semaphore_signal(barrier, inc=1, device_id=device((g + k) % groups, q), device_id_type=MESH)
        return 0

    lax.fori_loop(1, groups, greet, 0)
    for k in range(1, nlev):
        for offset in (-1, 0, 1):
            pl.semaphore_signal(barrier, inc=1, device_id=device(beside(offset), other(k)), device_id_type=MESH)
    pl.semaphore_wait(barrier, groups - 1 + 3 * (nlev - 1))

    for k in range(1, nlev):
        pltpu.make_async_remote_copy(
            src_ref=slot_ref, dst_ref=slots.at[q], send_sem=slot_send, recv_sem=slot_recv,
            device_id=device(g, other(k)), device_id_type=MESH,
        ).start()
    pltpu.make_async_copy(slot_ref, slots.at[q], slot_recv).start()

    for h in range(4):
        def send(i, _, h=h):
            target = ((high_at + h) % 4) * section + (low_at + i) % section
            pltpu.make_async_remote_copy(
                src_ref=msg_ref.at[target], dst_ref=arrived.at[g], send_sem=a2a_send, recv_sem=a2a_recv.at[h],
                device_id=device(target, q), device_id_type=MESH,
            ).start()
            return 0

        lax.fori_loop(1 if h == 0 else 0, section, send, 0)
    pltpu.make_async_copy(msg_ref.at[g], arrived.at[g], a2a_recv.at[0]).start()

    is_temp = q < 2
    half = q % 2
    edge_row = jnp.where(half == 0, jnp.where(is_temp, temp_ref[15:16, :], salt_ref[15:16, :]),
                         jnp.where(is_temp, temp_ref[0:1, :], salt_ref[0:1, :]))
    edge_from[...] = edge_row
    edge = pltpu.make_async_remote_copy(
        src_ref=edge_from, dst_ref=edge_to, send_sem=edge_send, recv_sem=edge_recv,
        device_id=device(beside(1 - 2 * half), q), device_id_type=MESH,
    )
    edge.start()

    pltpu.make_async_copy(slots, slots, slot_recv).wait()
    part_rows = parts.shape[2]
    ids = lax.broadcasted_iota(jnp.int32, (part_rows, slots.shape[2]), 0)
    for sec in range(3):
        for h in range(2):
            base = (sec * 2 + h) * part_rows
            total = None
            for k in range(nlev):
                hot = jnp.where(slots[k] == ids + base, 1.0, 0.0).astype(BF16)
                rows = slice(k * slots.shape[2], (k + 1) * slots.shape[2])
                term = jnp.dot(hot, high_ref[rows, :], preferred_element_type=F32)
                term += jnp.dot(hot, low_ref[rows, :], preferred_element_type=F32)
                total = term if total is None else total + term
            for f in range(2):
                parts[sec, f * 2 + h] = total[:, f * BLOCK : (f + 1) * BLOCK].astype(BF16)
    for sec in range(3):
        for k in range(nlev):
            if sec == 1 and k == 0:
                continue
            pltpu.make_async_remote_copy(
                src_ref=parts.at[sec, other(k)], dst_ref=sums.at[sec, q], send_sem=part_send, recv_sem=part_recv,
                device_id=device(beside(sec - 1), other(k)), device_id_type=MESH,
            ).start()
    pltpu.make_async_copy(parts.at[1, q], sums.at[1, q], part_recv).start()

    lanes = lax.broadcasted_iota(jnp.int32, (8, BLOCK), 1)

    def regroup_chunk(h):
        source = (high_at + 4 - h) % 4
        here = arrived.at[pl.ds(source * section, section)]
        pltpu.make_async_copy(here, here, a2a_recv.at[h]).wait()

        def tile(t, _):
            for i in range(3):
                out = [None] * (section * band // BLOCK)
                for b in range(section):
                    piece = arrived[source * section + b, :, pl.ds(pl.multiple_of(t * BLOCK, BLOCK), BLOCK)].astype(F32)
                    shift = (band * (b - i)) % BLOCK
                    if shift:
                        piece = pltpu.roll(piece, shift, 1)
                    at, begin = divmod(band * b, BLOCK)
                    if begin == 0:
                        out[at] = piece
                    else:
                        out[at] = jnp.where(lanes >= begin, piece, out[at])
                        if begin + band > BLOCK:
                            out[at + 1] = piece
                row = pl.multiple_of(t * 24 + i * 8, 8)
                for n, value in enumerate(out):
                    regroup[pl.ds(row, 8), n * BLOCK : (n + 1) * BLOCK] = value
            return 0

        lax.fori_loop(0, 4, tile, 0)
        gathered[q, h] = regroup[...].astype(BF16)
        for k, sem in ((1, left_recv), (3, right_recv)):
            pltpu.make_async_remote_copy(
                src_ref=gathered.at[q, h], dst_ref=gathered.at[q, h], send_sem=ring_send, recv_sem=sem.at[h],
                device_id=device(g, other(k)), device_id_type=MESH,
            ).start()

    split = gathered.shape[2] // 2

    def forward(h):
        for origin, target, sem, rows, far in (
            (3, 1, left_recv, slice(0, split), 0),
            (1, 3, right_recv, slice(split, 2 * split), 1),
        ):
            whole = gathered.at[other(origin), h]
            pltpu.make_async_copy(whole, whole, sem.at[h]).wait()
            some = gathered.at[other(origin), h, pl.ds(far * split, split)]
            pltpu.make_async_remote_copy(
                src_ref=some, dst_ref=some, send_sem=ring_send, recv_sem=far_recv.at[far, h],
                device_id=device(g, other(target)), device_id_type=MESH,
            ).start()

    regroup_chunk(0)
    regroup_chunk(1)

    pltpu.make_async_copy(sums, sums, part_recv).wait()
    forcing = None
    for sec in range(3):
        for k in range(nlev):
            term = sums[sec, k].astype(F32)
            forcing = term if forcing is None else forcing + term
    edge.wait()
    top = pl.multiple_of(half * 8, 8)
    value = jnp.where(is_temp, temp_ref[pl.ds(top, 8), :], salt_ref[pl.ds(top, 8), :])
    inner = jnp.where(half == 0, jnp.where(is_temp, temp_ref[8:9, :], salt_ref[8:9, :]),
                      jnp.where(is_temp, temp_ref[7:8, :], salt_ref[7:8, :]))
    outside = ((half == 0) & (g == 0)) | ((half == 1) & (g == groups - 1))
    outer = jnp.where(outside, 0.0, edge_to[...])
    above = jnp.where(half == 0, outer, inner)
    below = jnp.where(half == 0, inner, outer)
    cols = value.shape[1]
    rows8 = lax.broadcasted_iota(jnp.int32, value.shape, 0)
    north = jnp.where(rows8 == 0, jnp.broadcast_to(above, value.shape), pltpu.roll(value, 1, 0))
    south = jnp.where(rows8 == 7, jnp.broadcast_to(below, value.shape), pltpu.roll(value, 7, 0))
    laplace = south + north + pltpu.roll(value, 1, 1) + pltpu.roll(value, cols - 1, 1) - 4.0 * value
    moved = value + DIFFUSION * laplace
    sea = sea_ref[pl.ds(top, 8), :].astype(F32) * COUPLING
    for c in range(cols // BLOCK):
        new = moved[:, c * BLOCK : (c + 1) * BLOCK] + jnp.broadcast_to(sea[:, c : c + 1], (8, BLOCK)) * forcing[c * 8 : (c + 1) * 8]
        fresh[c * 8 : (c + 1) * 8, :] = new
    fresh_half[...] = fresh[...].astype(BF16)
    for k in range(1, nlev):
        pltpu.make_async_remote_copy(
            src_ref=fresh, dst_ref=near.at[q], send_sem=out_send, recv_sem=out_recv,
            device_id=device(g, other(k)), device_id_type=MESH,
        ).start()
    pltpu.make_async_copy(fresh, near.at[q], out_recv).start()

    @pl.when(is_temp)
    def _():
        for k in range(nlev):
            for side in range(2):
                pltpu.make_async_remote_copy(
                    src_ref=fresh_half, dst_ref=near_half.at[side, q], send_sem=half_send, recv_sem=half_recv,
                    device_id=device(beside(1 - 2 * side), other(k)), device_id_type=MESH,
                ).start()

    forward(0)
    regroup_chunk(2)
    forward(1)
    regroup_chunk(3)

    columns = want_ref.shape[0]
    perm = jnp.where(
        want_ref[...] == lax.broadcasted_iota(jnp.int32, (columns, columns), 1), 1.0, 0.0
    ).astype(BF16)

    def contract(h):
        for far, origin in ((0, 2), (1, 2)):
            some = gathered.at[other(origin), h, pl.ds(far * split, split)]
            pltpu.make_async_copy(some, some, far_recv.at[far, h]).wait()
        whole = jnp.concatenate([gathered[k, h] for k in range(nlev)], axis=0)
        ordered = jnp.dot(perm, whole, preferred_element_type=F32).astype(BF16)
        source = (high_at + 4 - h) % 4
        depth = section * band
        each = columns // 4
        for s in range(4):
            term = jnp.dot(
                ordered[s * each : (s + 1) * each],
                leg[s, pl.ds(pl.multiple_of(source * depth, 128), depth), :],
                preferred_element_type=F32,
            )
            spectra_ref[s] = term if h == 0 else spectra_ref[s] + term

    forward(2)
    leg_copy.wait()
    contract(0)
    forward(3)
    contract(1)

    pltpu.make_async_copy(near, near, out_recv).wait()
    pltpu.make_async_copy(near_half, near_half, half_recv).wait()
    for h in range(2):
        for c in range(cols // BLOCK):
            temp_out[h * 8 : (h + 1) * 8, c * BLOCK : (c + 1) * BLOCK] = near[h, c * 8 : (c + 1) * 8, :]
            salt_out[h * 8 : (h + 1) * 8, c * BLOCK : (c + 1) * BLOCK] = near[2 + h, c * 8 : (c + 1) * 8, :]
    mine = jnp.broadcast_to(slot_ref[...].astype(F32), (BLOCK, slot_ref.shape[1])).T
    blocks = surface_ref.shape[1] // BLOCK
    mine = mine[: blocks * band, :1]
    tiles = lax.broadcasted_iota(jnp.int32, (blocks * band, part_rows), 1).astype(F32)
    surface = None
    for sec in range(3):
        for h in range(2):
            hot = jnp.where(mine == tiles + float((sec * 2 + h) * part_rows), 1.0, 0.0).astype(BF16)
            if sec == 1:
                cells = near[h].astype(BF16)
            else:
                cells = near_half[sec // 2, h]
            term = jnp.dot(hot, cells, preferred_element_type=F32)
            surface = term if surface is None else surface + term
    row_lanes = lax.broadcasted_iota(jnp.int32, (1, BLOCK), 1)
    first_point = q * (blocks * BLOCK)
    for b in range(blocks):
        points = row_lanes + (first_point + b * BLOCK)
        keep = points < lat_ref[...]
        surface_ref[:, b * BLOCK : (b + 1) * BLOCK] = jnp.where(keep, surface[b * band : (b + 1) * band], 0.0)

    contract(2)
    contract(3)

    for k in range(1, nlev):
        pltpu.make_async_copy(slot_ref, slots.at[k], slot_send).wait()
    some = msg_ref.at[pl.ds(0, groups - 1)]
    pltpu.make_async_copy(some, some, a2a_send).wait()
    for k in range(3 * nlev - 1):
        pltpu.make_async_copy(parts.at[0, 0], sums.at[0, 0], part_send).wait()
    three = gathered.at[pl.ds(0, 3)]
    pltpu.make_async_copy(three, three, ring_send).wait()
    for k in range(1, nlev):
        pltpu.make_async_copy(fresh, near.at[0], out_send).wait()

    @pl.when(is_temp)
    def _():
        for k in range(2 * nlev):
            pltpu.make_async_copy(fresh_half, near_half.at[0, 0], half_send).wait()


def body(
    sizes,
    atmos_fields,
    lat_points,
    wave_order,
    legendre,
    column_weight,
    block_remap,
    ocean_temp,
    ocean_salt,
    sea_mask,
):
    nlat, nlev, nocn = sizes
    nf, nl, band, length = atmos_fields.shape
    g = lax.axis_index("lat") * nocn + lax.axis_index("ocn")
    orow, ocols = ocean_temp.shape
    tcols = ocols // BLOCK
    tile_count = orow * tcols
    part_rows = tile_count // 2
    local = block_remap - (g - 1) * tile_count
    sec, inside = local // tile_count, local % tile_count
    r, c = inside // tcols, inside % tcols
    slot = sec * tile_count + (r // 8) * part_rows + c * 8 + r % 8
    slot = slot.T.reshape(1, -1)
    slot = jnp.pad(slot, ((0, 0), (0, 512 - slot.shape[1])), constant_values=-1)
    msg, high, low = local_part(atmos_fields, lat_points, wave_order, column_weight)

    s, lev, f, c = np.meshgrid(np.arange(4), np.arange(nlev * nl), np.arange(nf), np.arange(2), indexing="ij")
    want = ((lev // nl) * nf * nl + f * nl + lev % nl) * 8 + c * 4 + s
    want = jnp.asarray(want.reshape(-1, 1), jnp.int32)

    each, nj, degrees = legendre.shape
    vm = pl.BlockSpec(memory_space=pltpu.VMEM)
    depth = nj // 4
    sem = pltpu.SemaphoreType.DMA
    quarter = length // nlev
    return pl.pallas_call(
        functools.partial(link_kernel, sizes),
        in_specs=[vm] * 9 + [pl.BlockSpec(memory_space=pl.ANY)],
        out_specs=[vm] * 4,
        out_shape=[
            jax.ShapeDtypeStruct((each, nlev * nl * nf * 2, degrees), F32),
            jax.ShapeDtypeStruct((orow, ocols), F32),
            jax.ShapeDtypeStruct((orow, ocols), F32),
            jax.ShapeDtypeStruct((band, quarter), F32),
        ],
        scratch_shapes=[
            pltpu.VMEM(legendre.shape, BF16),
            pltpu.VMEM(msg.shape, BF16),
            pltpu.VMEM((nlev, 4, nl * nf * 8, depth), BF16),
            pltpu.VMEM((nl * nf * 8, depth), F32),
            pltpu.VMEM((3, nlev, part_rows, BLOCK), BF16),
            pltpu.VMEM((3, nlev, part_rows, BLOCK), BF16),
            pltpu.VMEM((nlev, 1, 512), jnp.int32),
            pltpu.VMEM((1, ocols), F32),
            pltpu.VMEM((1, ocols), F32),
            pltpu.VMEM((part_rows, BLOCK), F32),
            pltpu.VMEM((part_rows, BLOCK), BF16),
            pltpu.VMEM((nlev, part_rows, BLOCK), F32),
            pltpu.VMEM((2, 2, part_rows, BLOCK), BF16),
            sem, sem, sem((4,)), sem, sem, sem, sem, sem, sem,
            sem, sem((4,)), sem((4,)), sem((2, 4)), sem, sem, sem, sem, sem,
        ],
        compiler_params=pltpu.CompilerParams(
            collective_id=0, has_side_effects=True, vmem_limit_bytes=40 * 1024 * 1024
        ),
    )(
        lat_points.reshape(band, 1), msg, high, low, slot, ocean_temp, ocean_salt, sea_mask, want, legendre,
    )


def solution(mesh):
    both = ("lat", "ocn")
    placed = (
        P(None, "lev", both, None),
        P(both),
        P(),
        P(both, None, "lev"),
        P(None, "lev"),
        P(both, "lev"),
        P(both, None),
        P(both, None),
        P(both, None),
    )
    sizes = tuple(mesh.shape[a] for a in ("lat", "lev", "ocn"))
    return jax.shard_map(
        functools.partial(body, sizes),
        mesh=mesh,
        in_specs=placed,
        out_specs=(P(both, None, "lev"), P(both, None), P(both, None), P(both, "lev")),
        check_vma=False,
    )
```

```python
import functools
import math

import jax
import jax.numpy as jnp
from jax import lax
from jax.experimental import pallas as pl
from jax.experimental.pallas import tpu as pltpu
from jax.sharding import PartitionSpec as P

BLOCK = 128
FULL_TURN = 2.0 * math.pi
DIFFUSION = 0.2
COUPLING = 0.5
CHUNK = 512
MESH = pl.DeviceIdType.MESH
F32 = jnp.float32
BF16 = jnp.bfloat16


def cos_sin(phase, length):
    quarter = length // 4
    turns = sum((phase >= quarter // 2 + i * quarter).astype(jnp.int32) for i in range(4))
    t = (phase - turns * quarter).astype(F32) * (FULL_TURN / length)
    u = t * t
    c = 1.0 + u * (-1 / 2 + u * (1 / 24 + u * (-1 / 720 + u * (1 / 40320 - u / 3628800))))
    s = t * (1.0 + u * (-1 / 6 + u * (1 / 120 + u * (-1 / 5040 + u * (1 / 362880)))))
    odd = (turns == 1) | (turns == 3)
    cos = jnp.where(odd, s, c)
    sin = jnp.where(odd, c, s)
    cos = jnp.where((turns == 1) | (turns == 2), -cos, cos)
    sin = jnp.where((turns == 2) | (turns == 3), -sin, sin)
    return cos, sin


def modulo(value, length):
    whole = jnp.floor((value.astype(F32) + 0.5) * (1.0 / length)).astype(jnp.int32)
    return value - whole * length


def fused_kernel(
    sizes,
    lat_hbm, wave_hbm, weight_hbm, remap_hbm, x_hbm, temp_hbm, salt_hbm, sea_hbm, leg_hbm,
    spectra_hbm, temp_to, salt_to, surface_to,
    spectra_ref, temp_out, salt_out, surface_ref, store_sem,
    lat_ref, wave_ref, weight_ref, remap_ref, x_ref, temp_ref, salt_ref, sea_ref, leg,
    table_a, table_b, acc, padded, blocks, block_pair, fine, coarse, lat_col, by_block_slots, slot_own, msg,
    arrived, gathered, regroup, parts, sums, slots, edge_from, edge_to, fresh, near, half_from, near_half,
    small_sem, x_sem, leg_sem, a2a_send, a2a_recv, slot_send, slot_recv, edge_send, edge_recv, part_send, part_recv,
    ring_send, left_recv, right_recv, far_recv, out_send, out_recv, half_send, half_recv,
):
    nlat, nlev, nocn = sizes
    groups = nlat * nocn
    lat_at, q, ocn_at = lax.axis_index("lat"), lax.axis_index("lev"), lax.axis_index("ocn")
    g = lat_at * nocn + ocn_at
    section = groups // 4
    high_at, low_at = g // section, g % section
    band = lat_hbm.shape[0]
    steps, rows, width = x_ref.shape
    waves = wave_ref.shape[1]
    pair_rows = 2 * band
    pairs = rows // pair_rows
    levels = rows // (2 * band)
    pieces = width // BLOCK
    length = steps * width
    count = length // BLOCK
    lane_blocks = count // nlev

    def device(group, lev):
        return (group // nocn, lev, group % nocn)

    def beside(offset):
        return (g + groups + offset) % groups

    def other(k):
        return (q + k) % nlev

    small = [
        pltpu.make_async_copy(a, b, small_sem.at[n])
        for n, (a, b) in enumerate(
            (
                (lat_hbm, lat_ref), (wave_hbm, wave_ref), (weight_hbm, weight_ref), (remap_hbm, remap_ref),
                (temp_hbm, temp_ref), (salt_hbm, salt_ref), (sea_hbm, sea_ref),
            )
        )
    ]
    for copy in small:
        copy.start()

    def x_copy(i):
        return pltpu.make_async_copy(
            x_hbm.at[:, pl.ds(pl.multiple_of(i * width, BLOCK), width)], x_ref.at[i], x_sem.at[i]
        )

    def start_x(i, _):
        x_copy(i).start()
        return 0

    lax.fori_loop(0, steps, start_x, 0)
    leg_copy = pltpu.make_async_copy(leg_hbm, leg, leg_sem)
    leg_copy.start()

    barrier = pltpu.get_barrier_semaphore()

    def greet(k, _):
        pl.semaphore_signal(barrier, inc=1, device_id=device((g + k) % groups, q), device_id_type=MESH)
        return 0

    lax.fori_loop(1, groups, greet, 0)
    for k in range(1, nlev):
        for offset in (-1, 0, 1):
            pl.semaphore_signal(barrier, inc=1, device_id=device(beside(offset), other(k)), device_id_type=MESH)

    for copy in small:
        copy.wait()
    for j in range(band):
        row = jnp.full((1, BLOCK), lat_ref[j], jnp.int32)
        lat_col[j : j + 1, :] = row
        lat_col[band + j : band + j + 1, :] = row
    wave = wave_ref[...]
    offsets = lax.broadcasted_iota(jnp.int32, (BLOCK, waves), 0)
    fine[0], fine[1] = cos_sin(modulo(offsets * wave, length), length)
    starts = lax.broadcasted_iota(jnp.int32, (count, waves), 0)
    coarse[0], coarse[1] = cos_sin(BLOCK * modulo(starts * wave, count), length)

    group = 3 * band
    tiles_row = slot_own.shape[1] // BLOCK
    per_lev = slot_own.shape[1]
    for k in range(nlev):
        for t in range(tiles_row):
            used = min(3, lane_blocks - 3 * t) * band
            start = k * per_lev + t * BLOCK + used
            blocks[start : k * per_lev + (t + 1) * BLOCK, :] = jnp.zeros((BLOCK - used, 2 * BLOCK), F32)

    orow, ocols = temp_ref.shape
    tcols = ocols // BLOCK
    tile_count = orow * tcols
    part_rows = tile_count // 2
    local = remap_ref[...] - (g - 1) * tile_count
    sec = (local >= tile_count).astype(jnp.int32) + (local >= 2 * tile_count).astype(jnp.int32)
    inside = local - sec * tile_count
    r = jnp.floor((inside.astype(F32) + 0.5) * (1.0 / tcols)).astype(jnp.int32)
    c = inside - r * tcols
    low_half = (r >= 8).astype(jnp.int32)
    slot = sec * tile_count + low_half * part_rows + c * 8 + r - 8 * low_half
    by_block_slots[...] = jnp.zeros(by_block_slots.shape, F32)
    by_block_slots[:lane_blocks, :band] = slot.astype(F32)
    by_block = by_block_slots[...]
    moved_slots = [by_block, pltpu.roll(by_block, band, 1), pltpu.roll(by_block, 2 * band, 1)]
    lane_row = lax.broadcasted_iota(jnp.int32, (1, BLOCK), 1)
    for t in range(tiles_row):
        row = jnp.full((1, BLOCK), -1.0, F32)
        for i in range(3):
            b = 3 * t + i
            if b < lane_blocks:
                here = (lane_row >= band * i) & (lane_row < band * (i + 1))
                row = jnp.where(here, moved_slots[i][b : b + 1], row)
        slot_own[:, t * BLOCK : (t + 1) * BLOCK] = row.astype(jnp.int32)

    pair_lanes = lax.broadcasted_iota(jnp.int32, (pair_rows, BLOCK), 1)
    upper = lax.broadcasted_iota(jnp.int32, (pair_rows, BLOCK), 0) < band
    weights = weight_ref[...].astype(F32)
    scales = [
        [
            jnp.where(upper, weights[f : f + 1, 2 * p : 2 * p + 1], weights[f : f + 1, 2 * p + 1 : 2 * p + 2])
            for p in range(pairs // 2)
        ]
        for f in range(2)
    ]

    def mask_step(step, _):
        x_copy(step).wait()
        for a in range(pieces):
            cols = slice(a * BLOCK, (a + 1) * BLOCK)
            keep = pair_lanes + (step * width + a * BLOCK) < lat_col[...]
            at = step * pieces + a
            inner = at % lane_blocks
            start = (at // lane_blocks) * per_lev + (inner // 3) * BLOCK + (inner % 3) * band
            start = pl.multiple_of(start, 8)
            for f in range(2):
                total = None
                for p in range(pairs // 2):
                    here = slice((f * (pairs // 2) + p) * pair_rows, (f * (pairs // 2) + p + 1) * pair_rows)
                    part = jnp.where(keep, x_ref[step, here, cols].astype(F32), 0.0)
                    x_ref[step, here, cols] = part.astype(BF16)
                    term = part * scales[f][p]
                    total = term if total is None else total + term
                blocks[pl.ds(start, band), f * BLOCK : (f + 1) * BLOCK] = total[:band] + total[band:]
        return 0

    early = 4
    lax.fori_loop(0, early, mask_step, 0)

    pl.semaphore_wait(barrier, groups - 1 + 3 * (nlev - 1))
    for k in range(1, nlev):
        pltpu.make_async_remote_copy(
            src_ref=slot_own, dst_ref=slots.at[q], send_sem=slot_send, recv_sem=slot_recv,
            device_id=device(g, other(k)), device_id_type=MESH,
        ).start()
    pltpu.make_async_copy(slot_own, slots.at[q], slot_recv).start()
    is_temp = q < 2
    half = q % 2
    edge_from[...] = jnp.where(
        half == 0,
        jnp.where(is_temp, temp_ref[orow - 1 : orow, :], salt_ref[orow - 1 : orow, :]),
        jnp.where(is_temp, temp_ref[0:1, :], salt_ref[0:1, :]),
    )
    edge = pltpu.make_async_remote_copy(
        src_ref=edge_from, dst_ref=edge_to, send_sem=edge_send, recv_sem=edge_recv,
        device_id=device(beside(1 - 2 * half), q), device_id_type=MESH,
    )
    edge.start()

    lax.fori_loop(early, steps, mask_step, 0)

    high = blocks[...].astype(BF16)
    block_pair[:, : 2 * BLOCK] = high
    block_pair[:, 2 * BLOCK :] = (blocks[...] - high.astype(F32)).astype(BF16)
    pltpu.make_async_copy(slots, slots, slot_recv).wait()
    all_slots = jnp.concatenate([slots[k] for k in range(nlev)], axis=1)
    ids = lax.broadcasted_iota(jnp.int32, (part_rows, all_slots.shape[1]), 0)
    for sec in range(3):
        for h in range(2):
            hot = jnp.where(all_slots == ids + (sec * 2 + h) * part_rows, 1.0, 0.0).astype(BF16)
            total = jnp.dot(hot, block_pair[...], preferred_element_type=F32)
            for f in range(2):
                both = total[:, f * BLOCK : (f + 1) * BLOCK] + total[:, (2 + f) * BLOCK : (3 + f) * BLOCK]
                parts[sec, f * 2 + h] = both.astype(BF16)
        for k in range(nlev):
            if sec == 1 and k == 0:
                continue
            pltpu.make_async_remote_copy(
                src_ref=parts.at[sec, other(k)], dst_ref=sums.at[sec, q], send_sem=part_send, recv_sem=part_recv,
                device_id=device(beside(sec - 1), other(k)), device_id_type=MESH,
            ).start()
    pltpu.make_async_copy(parts.at[1, q], sums.at[1, q], part_recv).start()

    def make_table(table, step):
        fc, fs = fine[0], fine[1]
        for a in range(pieces):
            cc = coarse[0, pl.ds(step * pieces + a, 1), :]
            cs = coarse[1, pl.ds(step * pieces + a, 1), :]
            table[a * BLOCK : (a + 1) * BLOCK, :waves] = (fc * cc - fs * cs).astype(BF16)
            table[a * BLOCK : (a + 1) * BLOCK, waves:] = (-(fs * cc) - fc * cs).astype(BF16)

    make_table(table_a, 0)
    acc[...] = jnp.zeros(acc.shape, F32)

    def two_steps(i, _):
        make_table(table_b, 2 * i + 1)
        acc[...] += jnp.dot(x_ref[2 * i], table_a[...], preferred_element_type=F32)
        make_table(table_a, 2 * i + 2)
        acc[...] += jnp.dot(x_ref[2 * i + 1], table_b[...], preferred_element_type=F32)
        return 0

    lax.fori_loop(0, steps // 2, two_steps, 0)
    acc[...] += jnp.dot(x_ref[steps - 1], table_a[...], preferred_element_type=F32)

    lat = lat_col[:band, :]
    root = 1.0 / jnp.sqrt(lat.astype(F32))
    for n in range(waves // BLOCK):
        weight = jnp.where(2 * wave_ref[:, n * BLOCK : (n + 1) * BLOCK] < lat, root, 0.0)
        for c in range(2):
            cols = slice(c * waves + n * BLOCK, c * waves + (n + 1) * BLOCK)
            for fl in range(rows // band):
                base = (fl // 3) * BLOCK + (fl % 3) * band
                padded[base : base + band, cols] = acc[fl * band : (fl + 1) * band, cols] * weight
    for t in range(rows // group):
        padded[t * BLOCK + group : (t + 1) * BLOCK, :] = jnp.zeros((BLOCK - group, 2 * waves), F32)
    turned = padded[...].T
    real = turned[:waves].reshape(waves // 8, 8, turned.shape[1])
    imag = turned[waves:].reshape(waves // 8, 8, turned.shape[1])
    first = lax.broadcasted_iota(jnp.int32, real.shape, 1) < 4
    even = jnp.where(first, real, pltpu.roll(imag, 4, 1))
    odd = jnp.where(first, pltpu.roll(real, 4, 1), imag)
    msg[...] = jnp.stack([even, odd], axis=1).reshape(msg.shape).astype(BF16)

    for h in range(4):
        def send(i, _, h=h):
            target = ((high_at + h) % 4) * section + (low_at + i) % section
            pltpu.make_async_remote_copy(
                src_ref=msg.at[target], dst_ref=arrived.at[g], send_sem=a2a_send, recv_sem=a2a_recv.at[h],
                device_id=device(target, q), device_id_type=MESH,
            ).start()
            return 0

        lax.fori_loop(1 if h == 0 else 0, section, send, 0)
    pltpu.make_async_copy(msg.at[g], arrived.at[g], a2a_recv.at[0]).start()

    pltpu.make_async_copy(sums, sums, part_recv).wait()
    forcing = None
    for sec in range(3):
        for k in range(nlev):
            term = sums[sec, k].astype(F32)
            forcing = term if forcing is None else forcing + term
    edge.wait()
    top = pl.multiple_of(half * 8, 8)
    value = jnp.where(is_temp, temp_ref[pl.ds(top, 8), :], salt_ref[pl.ds(top, 8), :])
    inner = jnp.where(
        half == 0,
        jnp.where(is_temp, temp_ref[8:9, :], salt_ref[8:9, :]),
        jnp.where(is_temp, temp_ref[7:8, :], salt_ref[7:8, :]),
    )
    outside = ((half == 0) & (g == 0)) | ((half == 1) & (g == groups - 1))
    outer = jnp.where(outside, 0.0, edge_to[...])
    above = jnp.where(half == 0, outer, inner)
    below = jnp.where(half == 0, inner, outer)
    rows8 = lax.broadcasted_iota(jnp.int32, value.shape, 0)
    north = jnp.where(rows8 == 0, jnp.broadcast_to(above, value.shape), pltpu.roll(value, 1, 0))
    south = jnp.where(rows8 == 7, jnp.broadcast_to(below, value.shape), pltpu.roll(value, 7, 0))
    laplace = south + north + pltpu.roll(value, 1, 1) + pltpu.roll(value, ocols - 1, 1) - 4.0 * value
    moved = value + DIFFUSION * laplace
    sea = sea_ref[pl.ds(top, 8), :].astype(F32) * COUPLING
    for c in range(tcols):
        here = slice(c * 8, (c + 1) * 8)
        fresh[here, :] = (
            moved[:, c * BLOCK : (c + 1) * BLOCK] + jnp.broadcast_to(sea[:, c : c + 1], (8, BLOCK)) * forcing[here]
        )
    for k in range(1, nlev):
        pltpu.make_async_remote_copy(
            src_ref=fresh, dst_ref=near.at[q], send_sem=out_send, recv_sem=out_recv,
            device_id=device(g, other(k)), device_id_type=MESH,
        ).start()
    pltpu.make_async_copy(fresh, near.at[q], out_recv).start()

    lanes = lax.broadcasted_iota(jnp.int32, (8, BLOCK), 1)

    def regroup_chunk(h):
        source = (high_at + 4 - h) % 4
        here = arrived.at[pl.ds(source * section, section)]
        pltpu.make_async_copy(here, here, a2a_recv.at[h]).wait()

        def tile(t, _):
            for i in range(3):
                out = [None] * (section * band // BLOCK)
                for b in range(section):
                    piece = arrived[source * section + b, :, pl.ds(pl.multiple_of(t * BLOCK, BLOCK), BLOCK)].astype(F32)
                    shift = (band * (b - i)) % BLOCK
                    if shift:
                        piece = pltpu.roll(piece, shift, 1)
                    at, begin = divmod(band * b, BLOCK)
                    if begin == 0:
                        out[at] = piece
                    else:
                        out[at] = jnp.where(lanes >= begin, piece, out[at])
                        if begin + band > BLOCK:
                            out[at + 1] = piece
                row = pl.multiple_of(t * 24 + i * 8, 8)
                for n, tile_value in enumerate(out):
                    regroup[pl.ds(row, 8), n * BLOCK : (n + 1) * BLOCK] = tile_value
            return 0

        lax.fori_loop(0, 4, tile, 0)
        gathered[q, h] = regroup[...].astype(BF16)
        for k, sem in ((1, left_recv), (3, right_recv)):
            pltpu.make_async_remote_copy(
                src_ref=gathered.at[q, h], dst_ref=gathered.at[q, h], send_sem=ring_send, recv_sem=sem.at[h],
                device_id=device(g, other(k)), device_id_type=MESH,
            ).start()

    split = gathered.shape[2] // 2

    def forward(h):
        for origin, target, sem, far in ((3, 1, left_recv, 0), (1, 3, right_recv, 1)):
            whole = gathered.at[other(origin), h]
            pltpu.make_async_copy(whole, whole, sem.at[h]).wait()
            some = gathered.at[other(origin), h, pl.ds(far * split, split)]
            pltpu.make_async_remote_copy(
                src_ref=some, dst_ref=some, send_sem=ring_send, recv_sem=far_recv.at[far, h],
                device_id=device(g, other(target)), device_id_type=MESH,
            ).start()

    regroup_chunk(0)
    regroup_chunk(1)
    forward(0)

    pltpu.make_async_copy(near, near, out_recv).wait()
    half_from[...] = near[:2].astype(BF16)
    for side in range(2):
        pltpu.make_async_remote_copy(
            src_ref=half_from, dst_ref=near_half.at[side], send_sem=half_send, recv_sem=half_recv,
            device_id=device(beside(1 - 2 * side), q), device_id_type=MESH,
        ).start()
    regroup_chunk(2)
    forward(1)
    regroup_chunk(3)
    for h in range(2):
        for c in range(tcols):
            cols = slice(c * BLOCK, (c + 1) * BLOCK)
            temp_out[h * 8 : (h + 1) * 8, cols] = near[h, c * 8 : (c + 1) * 8, :]
            salt_out[h * 8 : (h + 1) * 8, cols] = near[2 + h, c * 8 : (c + 1) * 8, :]

    columns = nlev * gathered.shape[2]
    each = columns // 4
    at = lax.broadcasted_iota(jnp.int32, (columns, 1), 0)
    s = sum((at >= n * each).astype(jnp.int32) for n in range(1, 4))
    rest = at - s * each
    lev_rows = 4 * levels
    from_q = sum((rest >= n * lev_rows).astype(jnp.int32) for n in range(1, nlev))
    rest = rest - from_q * lev_rows
    lev = rest // 4
    f, c = (rest // 2) % 2, rest % 2
    want = from_q * (16 * levels) + (f * levels + lev) * 8 + c * 4 + s
    perm = jnp.where(want == lax.broadcasted_iota(jnp.int32, (columns, columns), 1), 1.0, 0.0).astype(BF16)

    def contract(h):
        for far in range(2):
            some = gathered.at[other(2), h, pl.ds(far * split, split)]
            pltpu.make_async_copy(some, some, far_recv.at[far, h]).wait()
        whole = jnp.concatenate([gathered[k, h] for k in range(nlev)], axis=0)
        ordered = jnp.dot(perm, whole, preferred_element_type=F32).astype(BF16)
        source = (high_at + 4 - h) % 4
        depth = section * band
        for s in range(4):
            term = jnp.dot(
                ordered[s * each : (s + 1) * each],
                leg[s, pl.ds(pl.multiple_of(source * depth, BLOCK), depth), :],
                preferred_element_type=F32,
            )
            spectra_ref[s] = term if h == 0 else spectra_ref[s] + term

    forward(2)
    leg_copy.wait()
    contract(0)
    forward(3)
    contract(1)

    pltpu.make_async_copy(near_half, near_half, half_recv).wait()
    mine = jnp.broadcast_to(slot_own[...].astype(F32), (BLOCK, per_lev)).T[:, :1]
    tiles = lax.broadcasted_iota(jnp.int32, (per_lev, part_rows), 1).astype(F32)
    surface = None
    for sec in range(3):
        for h in range(2):
            hot = jnp.where(mine == tiles + float((sec * 2 + h) * part_rows), 1.0, 0.0).astype(BF16)
            cells = near[h].astype(BF16) if sec == 1 else near_half[sec // 2, h]
            term = jnp.dot(hot, cells, preferred_element_type=F32)
            surface = term if surface is None else surface + term
    first_lane = lax.broadcasted_iota(jnp.int32, (band, BLOCK), 1)
    for b in range(lane_blocks):
        points = first_lane + (q * lane_blocks + b) * BLOCK
        base = (b // 3) * BLOCK + (b % 3) * band
        surface_ref[:, b * BLOCK : (b + 1) * BLOCK] = jnp.where(
            points < lat_col[:band, :], surface[base : base + band], 0.0
        )

    stores = [
        pltpu.make_async_copy(a, b, store_sem.at[n])
        for n, (a, b) in enumerate(
            ((temp_out, temp_to), (salt_out, salt_to), (surface_ref, surface_to), (spectra_ref, spectra_hbm))
        )
    ]
    for store in stores[:3]:
        store.start()
    contract(2)
    contract(3)
    stores[3].start()
    for store in stores:
        store.wait()

    for k in range(1, nlev):
        pltpu.make_async_copy(slot_own, slots.at[k], slot_send).wait()
    some = msg.at[pl.ds(0, groups - 1)]
    pltpu.make_async_copy(some, some, a2a_send).wait()
    for k in range(3 * nlev - 1):
        pltpu.make_async_copy(parts.at[0, 0], sums.at[0, 0], part_send).wait()
    three = gathered.at[pl.ds(0, 3)]
    pltpu.make_async_copy(three, three, ring_send).wait()
    for k in range(1, nlev):
        pltpu.make_async_copy(fresh, near.at[0], out_send).wait()
    for side in range(2):
        pltpu.make_async_copy(half_from, near_half.at[0], half_send).wait()


def store_kernel(*refs):
    count = len(refs) // 2
    for n in range(count):
        refs[count + n][...] = refs[n][...]


def body(
    sizes,
    atmos_fields,
    lat_points,
    wave_order,
    legendre,
    column_weight,
    block_remap,
    ocean_temp,
    ocean_salt,
    sea_mask,
):
    nlat, nlev, nocn = sizes
    nf, nl, band, length = atmos_fields.shape
    groups = nlat * nocn
    rows = nf * nl * band
    waves = wave_order.shape[0]
    orow, ocols = ocean_temp.shape
    part_rows = orow * ocols // BLOCK // 2
    each, nj, degrees = legendre.shape
    depth = nj // 4
    quarter = length // nlev
    lanes = rows // (3 * band) * BLOCK
    per_lev = -(-(quarter // BLOCK) // 3) * BLOCK
    steps = length // CHUNK
    hbm = pl.BlockSpec(memory_space=pltpu.HBM)
    sem = pltpu.SemaphoreType.DMA
    outs = [
        jax.ShapeDtypeStruct((each, nlev * nl * nf * 2, degrees), F32),
        jax.ShapeDtypeStruct((orow, ocols), F32),
        jax.ShapeDtypeStruct((orow, ocols), F32),
        jax.ShapeDtypeStruct((band, quarter), F32),
    ]
    results = pl.pallas_call(
        functools.partial(fused_kernel, sizes),
        in_specs=[hbm] * 9,
        out_specs=[hbm] * 4,
        out_shape=outs,
        scratch_shapes=[pltpu.VMEM(o.shape, F32) for o in outs]
        + [
            sem((4,)),
            pltpu.SMEM((band,), jnp.int32),
            pltpu.VMEM((1, waves), jnp.int32),
            pltpu.VMEM(column_weight.shape, BF16),
            pltpu.VMEM(block_remap.shape[::-1], jnp.int32),
            pltpu.VMEM((steps, rows, CHUNK), BF16),
            pltpu.VMEM((orow, ocols), F32),
            pltpu.VMEM((orow, ocols), F32),
            pltpu.VMEM(sea_mask.shape, jnp.int32),
            pltpu.VMEM(legendre.shape, BF16),
            pltpu.VMEM((CHUNK, 2 * waves), BF16),
            pltpu.VMEM((CHUNK, 2 * waves), BF16),
            pltpu.VMEM((rows, 2 * waves), F32),
            pltpu.VMEM((lanes, 2 * waves), F32),
            pltpu.VMEM((nlev * per_lev, 2 * BLOCK), F32),
            pltpu.VMEM((nlev * per_lev, 4 * BLOCK), BF16),
            pltpu.VMEM((2, BLOCK, waves), F32),
            pltpu.VMEM((2, length // BLOCK, waves), F32),
            pltpu.VMEM((2 * band, BLOCK), jnp.int32),
            pltpu.VMEM((16, BLOCK), F32),
            pltpu.VMEM((1, per_lev), jnp.int32),
            pltpu.VMEM((groups, 2 * each, lanes), BF16),
            pltpu.VMEM((groups, 2 * each, lanes), BF16),
            pltpu.VMEM((nlev, 4, nl * nf * 8, depth), BF16),
            pltpu.VMEM((nl * nf * 8, depth), F32),
            pltpu.VMEM((3, nlev, part_rows, BLOCK), BF16),
            pltpu.VMEM((3, nlev, part_rows, BLOCK), BF16),
            pltpu.VMEM((nlev, 1, per_lev), jnp.int32),
            pltpu.VMEM((1, ocols), F32),
            pltpu.VMEM((1, ocols), F32),
            pltpu.VMEM((part_rows, BLOCK), F32),
            pltpu.VMEM((nlev, part_rows, BLOCK), F32),
            pltpu.VMEM((2, part_rows, BLOCK), BF16),
            pltpu.VMEM((2, 2, part_rows, BLOCK), BF16),
            sem((7,)), sem((steps,)), sem, sem, sem((4,)), sem, sem, sem, sem, sem, sem,
            sem, sem((4,)), sem((4,)), sem((2, 4)), sem, sem, sem, sem,
        ],
        compiler_params=pltpu.CompilerParams(
            collective_id=0, has_side_effects=True, vmem_limit_bytes=62 * 1024 * 1024
        ),
    )(
        lat_points, wave_order.reshape(1, waves), column_weight, block_remap.T, atmos_fields.reshape(rows, length),
        ocean_temp, ocean_salt, sea_mask, legendre,
    )
    return pl.pallas_call(store_kernel, out_shape=outs)(*results)


def solution(mesh):
    both = ("lat", "ocn")
    placed = (
        P(None, "lev", both, None),
        P(both),
        P(),
        P(both, None, "lev"),
        P(None, "lev"),
        P(both, "lev"),
        P(both, None),
        P(both, None),
        P(both, None),
    )
    sizes = tuple(mesh.shape[a] for a in ("lat", "lev", "ocn"))
    return jax.shard_map(
        functools.partial(body, sizes),
        mesh=mesh,
        in_specs=placed,
        out_specs=(P(both, None, "lev"), P(both, None), P(both, None), P(both, "lev")),
        check_vma=False,
    )
```

```python
import functools
import math

import jax
import jax.numpy as jnp
from jax import lax
from jax.experimental import pallas as pl
from jax.experimental.pallas import tpu as pltpu
from jax.sharding import PartitionSpec as P

BLOCK = 128
FULL_TURN = 2.0 * math.pi
DIFFUSION = 0.2
COUPLING = 0.5
CHUNK = 512
MESH = pl.DeviceIdType.MESH
F32 = jnp.float32
BF16 = jnp.bfloat16


def cos_sin(phase, length):
    quarter = length // 4
    turns = sum((phase >= quarter // 2 + i * quarter).astype(jnp.int32) for i in range(4))
    t = (phase - turns * quarter).astype(F32) * (FULL_TURN / length)
    u = t * t
    c = 1.0 + u * (-1 / 2 + u * (1 / 24 + u * (-1 / 720 + u * (1 / 40320 - u / 3628800))))
    s = t * (1.0 + u * (-1 / 6 + u * (1 / 120 + u * (-1 / 5040 + u * (1 / 362880)))))
    odd = (turns == 1) | (turns == 3)
    cos = jnp.where(odd, s, c)
    sin = jnp.where(odd, c, s)
    cos = jnp.where((turns == 1) | (turns == 2), -cos, cos)
    sin = jnp.where((turns == 2) | (turns == 3), -sin, sin)
    return cos, sin


def modulo(value, length):
    whole = jnp.floor((value.astype(F32) + 0.5) * (1.0 / length)).astype(jnp.int32)
    return value - whole * length


def fused_kernel(
    sizes,
    lat_hbm, wave_hbm, weight_hbm, remap_hbm, x_hbm, temp_hbm, salt_hbm, sea_hbm, leg_hbm,
    spectra_hbm, temp_to, salt_to, surface_to,
    spectra_ref, temp_out, salt_out, surface_ref, store_sem,
    lat_ref, wave_ref, weight_ref, remap_ref, x_ref, temp_ref, salt_ref, sea_ref, leg,
    table_a, table_b, acc, padded, blocks, block_pair, fine, coarse, lat_col, by_block_slots, slot_own, msg,
    arrived, gathered, regroup, parts, sums, slots, edge_from, edge_to, fresh, near, half_from, near_half,
    small_sem, x_sem, leg_sem, a2a_send, a2a_recv, slot_send, slot_recv, edge_send, edge_recv, part_send, part_recv,
    ring_send, left_recv, right_recv, far_recv, out_send, out_recv, half_send, half_recv,
):
    nlat, nlev, nocn = sizes
    groups = nlat * nocn
    lat_at, q, ocn_at = lax.axis_index("lat"), lax.axis_index("lev"), lax.axis_index("ocn")
    g = lat_at * nocn + ocn_at
    section = groups // 4
    lat_section = nlat // 4
    high_at, low_lat = lax.div(lat_at, lat_section), lax.rem(lat_at, lat_section)
    band = lat_hbm.shape[0]
    steps, rows, width = x_ref.shape
    waves = wave_ref.shape[1]
    pair_rows = 2 * band
    pairs = rows // pair_rows
    levels = rows // (2 * band)
    pieces = width // BLOCK
    length = steps * width
    count = length // BLOCK
    lane_blocks = count // nlev

    around = {-1: lax.rem(g + groups - 1, groups), 0: g, 1: lax.rem(g + 1, groups)}
    place = {n: (lax.div(v, nocn), lax.rem(v, nocn)) for n, v in around.items()}
    others = [lax.rem(q + k, nlev) for k in range(nlev)]
    ocns = [lax.rem(ocn_at + o, nocn) for o in range(nocn)]

    def beside(offset, lev):
        lat, ocn = place[offset]
        return (lat, lev, ocn)

    def across(up):
        return (jnp.where(up, place[1][0], place[-1][0]), q, jnp.where(up, place[1][1], place[-1][1]))

    def other(k):
        return others[k]

    small = [
        pltpu.make_async_copy(a, b, small_sem.at[n])
        for n, (a, b) in enumerate(
            (
                (lat_hbm, lat_ref), (wave_hbm, wave_ref), (weight_hbm, weight_ref), (remap_hbm, remap_ref),
                (temp_hbm, temp_ref), (salt_hbm, salt_ref), (sea_hbm, sea_ref),
            )
        )
    ]
    for copy in small:
        copy.start()

    def x_copy(i):
        return pltpu.make_async_copy(
            x_hbm.at[:, pl.ds(pl.multiple_of(i * width, BLOCK), width)], x_ref.at[i], x_sem.at[i]
        )

    def start_x(i, _):
        x_copy(i).start()
        return 0

    lax.fori_loop(0, steps, start_x, 0)
    leg_copy = pltpu.make_async_copy(leg_hbm, leg, leg_sem)

    barrier = pltpu.get_barrier_semaphore()

    def greet(i, _):
        lat = lax.rem(lat_at + i, nlat)
        for o in range(nocn):
            pl.semaphore_signal(barrier, inc=1, device_id=(lat, q, ocns[o]), device_id_type=MESH)
        return 0

    for o in range(1, nocn):
        pl.semaphore_signal(barrier, inc=1, device_id=(lat_at, q, ocns[o]), device_id_type=MESH)
    lax.fori_loop(1, nlat, greet, 0)
    for k in range(1, nlev):
        for offset in (-1, 0, 1):
            pl.semaphore_signal(barrier, inc=1, device_id=beside(offset, other(k)), device_id_type=MESH)

    for copy in small:
        copy.wait()
    for j in range(band):
        row = jnp.full((1, BLOCK), lat_ref[j], jnp.int32)
        lat_col[j : j + 1, :] = row
        lat_col[band + j : band + j + 1, :] = row
    wave = wave_ref[...]
    offsets = lax.broadcasted_iota(jnp.int32, (BLOCK, waves), 0)
    fine[0], fine[1] = cos_sin(modulo(offsets * wave, length), length)
    starts = lax.broadcasted_iota(jnp.int32, (count, waves), 0)
    coarse[0], coarse[1] = cos_sin(BLOCK * modulo(starts * wave, count), length)

    group = 3 * band
    tiles_row = slot_own.shape[1] // BLOCK
    per_lev = slot_own.shape[1]
    for k in range(nlev):
        for t in range(tiles_row):
            used = min(3, lane_blocks - 3 * t) * band
            start = k * per_lev + t * BLOCK + used
            blocks[start : k * per_lev + (t + 1) * BLOCK, :] = jnp.zeros((BLOCK - used, 2 * BLOCK), F32)

    orow, ocols = temp_ref.shape
    tcols = ocols // BLOCK
    tile_count = orow * tcols
    part_rows = tile_count // 2
    local = remap_ref[...] - (g - 1) * tile_count
    sec = (local >= tile_count).astype(jnp.int32) + (local >= 2 * tile_count).astype(jnp.int32)
    inside = local - sec * tile_count
    r = jnp.floor((inside.astype(F32) + 0.5) * (1.0 / tcols)).astype(jnp.int32)
    c = inside - r * tcols
    low_half = (r >= 8).astype(jnp.int32)
    slot = sec * tile_count + low_half * part_rows + c * 8 + r - 8 * low_half
    by_block_slots[...] = jnp.zeros(by_block_slots.shape, F32)
    by_block_slots[:lane_blocks, :band] = slot.astype(F32)
    by_block = by_block_slots[...]
    moved_slots = [by_block, pltpu.roll(by_block, band, 1), pltpu.roll(by_block, 2 * band, 1)]
    lane_row = lax.broadcasted_iota(jnp.int32, (1, BLOCK), 1)
    for t in range(tiles_row):
        row = jnp.full((1, BLOCK), -1.0, F32)
        for i in range(3):
            b = 3 * t + i
            if b < lane_blocks:
                here = (lane_row >= band * i) & (lane_row < band * (i + 1))
                row = jnp.where(here, moved_slots[i][b : b + 1], row)
        slot_own[:, t * BLOCK : (t + 1) * BLOCK] = row.astype(jnp.int32)

    pair_lanes = lax.broadcasted_iota(jnp.int32, (pair_rows, BLOCK), 1)
    upper = lax.broadcasted_iota(jnp.int32, (pair_rows, BLOCK), 0) < band
    weights = weight_ref[...].astype(F32)
    scales = [
        [
            jnp.where(upper, weights[f : f + 1, 2 * p : 2 * p + 1], weights[f : f + 1, 2 * p + 1 : 2 * p + 2])
            for p in range(pairs // 2)
        ]
        for f in range(2)
    ]

    def mask_step(step, _):
        x_copy(step).wait()
        for a in range(pieces):
            cols = slice(a * BLOCK, (a + 1) * BLOCK)
            keep = pair_lanes + (step * width + a * BLOCK) < lat_col[...]
            at = step * pieces + a
            inner = at % lane_blocks
            start = (at // lane_blocks) * per_lev + (inner // 3) * BLOCK + (inner % 3) * band
            start = pl.multiple_of(start, 8)
            for f in range(2):
                total = None
                for p in range(pairs // 2):
                    here = slice((f * (pairs // 2) + p) * pair_rows, (f * (pairs // 2) + p + 1) * pair_rows)
                    part = jnp.where(keep, x_ref[step, here, cols].astype(F32), 0.0)
                    x_ref[step, here, cols] = part.astype(BF16)
                    term = part * scales[f][p]
                    total = term if total is None else total + term
                blocks[pl.ds(start, band), f * BLOCK : (f + 1) * BLOCK] = total[:band] + total[band:]
        return 0

    early = 4
    lax.fori_loop(0, early, mask_step, 0)

    pl.semaphore_wait(barrier, groups - 1 + 3 * (nlev - 1))
    for k in range(1, nlev):
        pltpu.make_async_remote_copy(
            src_ref=slot_own, dst_ref=slots.at[q], send_sem=slot_send, recv_sem=slot_recv,
            device_id=beside(0, other(k)), device_id_type=MESH,
        ).start()
    pltpu.make_async_copy(slot_own, slots.at[q], slot_recv).start()
    is_temp = q < 2
    half = q % 2
    edge_from[...] = jnp.where(
        half == 0,
        jnp.where(is_temp, temp_ref[orow - 1 : orow, :], salt_ref[orow - 1 : orow, :]),
        jnp.where(is_temp, temp_ref[0:1, :], salt_ref[0:1, :]),
    )
    edge = pltpu.make_async_remote_copy(
        src_ref=edge_from, dst_ref=edge_to, send_sem=edge_send, recv_sem=edge_recv,
        device_id=across(half == 0), device_id_type=MESH,
    )
    edge.start()

    lax.fori_loop(early, steps, mask_step, 0)
    leg_copy.start()

    high = blocks[...].astype(BF16)
    block_pair[:, : 2 * BLOCK] = high
    block_pair[:, 2 * BLOCK :] = (blocks[...] - high.astype(F32)).astype(BF16)
    pltpu.make_async_copy(slots, slots, slot_recv).wait()
    all_slots = jnp.concatenate([slots[k] for k in range(nlev)], axis=1)
    ids = lax.broadcasted_iota(jnp.int32, (part_rows, all_slots.shape[1]), 0)
    for sec in range(3):
        for h in range(2):
            hot = jnp.where(all_slots == ids + (sec * 2 + h) * part_rows, 1.0, 0.0).astype(BF16)
            total = jnp.dot(hot, block_pair[...], preferred_element_type=F32)
            for f in range(2):
                both = total[:, f * BLOCK : (f + 1) * BLOCK] + total[:, (2 + f) * BLOCK : (3 + f) * BLOCK]
                parts[sec, f * 2 + h] = both.astype(BF16)
        for k in range(nlev):
            if sec == 1 and k == 0:
                continue
            pltpu.make_async_remote_copy(
                src_ref=parts.at[sec, other(k)], dst_ref=sums.at[sec, q], send_sem=part_send, recv_sem=part_recv,
                device_id=beside(sec - 1, other(k)), device_id_type=MESH,
            ).start()
    pltpu.make_async_copy(parts.at[1, q], sums.at[1, q], part_recv).start()

    def make_table(table, step):
        fc, fs = fine[0], fine[1]
        for a in range(pieces):
            cc = coarse[0, pl.ds(step * pieces + a, 1), :]
            cs = coarse[1, pl.ds(step * pieces + a, 1), :]
            table[a * BLOCK : (a + 1) * BLOCK, :waves] = (fc * cc - fs * cs).astype(BF16)
            table[a * BLOCK : (a + 1) * BLOCK, waves:] = (-(fs * cc) - fc * cs).astype(BF16)

    make_table(table_a, 0)
    acc[...] = jnp.zeros(acc.shape, F32)

    def two_steps(i, _):
        make_table(table_b, 2 * i + 1)
        acc[...] += jnp.dot(x_ref[2 * i], table_a[...], preferred_element_type=F32)
        make_table(table_a, 2 * i + 2)
        acc[...] += jnp.dot(x_ref[2 * i + 1], table_b[...], preferred_element_type=F32)
        return 0

    lax.fori_loop(0, steps // 2, two_steps, 0)
    acc[...] += jnp.dot(x_ref[steps - 1], table_a[...], preferred_element_type=F32)

    lat = lat_col[:band, :]
    root = 1.0 / jnp.sqrt(lat.astype(F32))
    for n in range(waves // BLOCK):
        weight = jnp.where(2 * wave_ref[:, n * BLOCK : (n + 1) * BLOCK] < lat, root, 0.0)
        for c in range(2):
            cols = slice(c * waves + n * BLOCK, c * waves + (n + 1) * BLOCK)
            for fl in range(rows // band):
                base = (fl // 3) * BLOCK + (fl % 3) * band
                padded[base : base + band, cols] = acc[fl * band : (fl + 1) * band, cols] * weight
    for t in range(rows // group):
        padded[t * BLOCK + group : (t + 1) * BLOCK, :] = jnp.zeros((BLOCK - group, 2 * waves), F32)
    turned = padded[...].T
    real = turned[:waves].reshape(waves // 8, 8, turned.shape[1])
    imag = turned[waves:].reshape(waves // 8, 8, turned.shape[1])
    first = lax.broadcasted_iota(jnp.int32, real.shape, 1) < 4
    even = jnp.where(first, real, pltpu.roll(imag, 4, 1))
    odd = jnp.where(first, pltpu.roll(real, 4, 1), imag)
    msg[...] = jnp.stack([even, odd], axis=1).reshape(msg.shape).astype(BF16)

    def send_group(n):
        h, first = n // 2, n % 2 * (lat_section // 2)
        high = lax.rem(high_at + h, 4)
        for a in range(first, first + lat_section // 2):
            lat_to = high * lat_section + lax.rem(low_lat + a, lat_section)
            for o in range(nocn):
                if h or a or o:
                    pltpu.make_async_remote_copy(
                        src_ref=msg.at[lat_to * nocn + ocns[o]], dst_ref=arrived.at[g],
                        send_sem=a2a_send.at[n], recv_sem=a2a_recv.at[h],
                        device_id=(lat_to, q, ocns[o]), device_id_type=MESH,
                    ).start()

    def wait_group(n):
        some = msg.at[pl.ds(0, section // 2 - (n == 0))]
        pltpu.make_async_copy(some, some, a2a_send.at[n]).wait()

    pltpu.make_async_copy(msg.at[g], arrived.at[g], a2a_recv.at[0]).start()
    send_group(0)
    send_group(1)
    send_group(2)
    send_group(3)

    pltpu.make_async_copy(sums, sums, part_recv).wait()
    forcing = None
    for sec in range(3):
        for k in range(nlev):
            term = sums[sec, k].astype(F32)
            forcing = term if forcing is None else forcing + term
    edge.wait()
    top = pl.multiple_of(half * 8, 8)
    value = jnp.where(is_temp, temp_ref[pl.ds(top, 8), :], salt_ref[pl.ds(top, 8), :])
    inner = jnp.where(
        half == 0,
        jnp.where(is_temp, temp_ref[8:9, :], salt_ref[8:9, :]),
        jnp.where(is_temp, temp_ref[7:8, :], salt_ref[7:8, :]),
    )
    outside = ((half == 0) & (g == 0)) | ((half == 1) & (g == groups - 1))
    outer = jnp.where(outside, 0.0, edge_to[...])
    above = jnp.where(half == 0, outer, inner)
    below = jnp.where(half == 0, inner, outer)
    rows8 = lax.broadcasted_iota(jnp.int32, value.shape, 0)
    north = jnp.where(rows8 == 0, jnp.broadcast_to(above, value.shape), pltpu.roll(value, 1, 0))
    south = jnp.where(rows8 == 7, jnp.broadcast_to(below, value.shape), pltpu.roll(value, 7, 0))
    laplace = south + north + pltpu.roll(value, 1, 1) + pltpu.roll(value, ocols - 1, 1) - 4.0 * value
    moved = value + DIFFUSION * laplace
    sea = sea_ref[pl.ds(top, 8), :].astype(F32) * COUPLING
    for c in range(tcols):
        here = slice(c * 8, (c + 1) * 8)
        fresh[here, :] = (
            moved[:, c * BLOCK : (c + 1) * BLOCK] + jnp.broadcast_to(sea[:, c : c + 1], (8, BLOCK)) * forcing[here]
        )
    for k in range(1, nlev):
        pltpu.make_async_remote_copy(
            src_ref=fresh, dst_ref=near.at[q], send_sem=out_send, recv_sem=out_recv,
            device_id=beside(0, other(k)), device_id_type=MESH,
        ).start()
    pltpu.make_async_copy(fresh, near.at[q], out_recv).start()

    lanes = lax.broadcasted_iota(jnp.int32, (8, BLOCK), 1)

    def regroup_chunk(h):
        source = lax.rem(high_at + 4 - h, 4)
        here = arrived.at[pl.ds(source * section, section)]
        pltpu.make_async_copy(here, here, a2a_recv.at[h]).wait()

        def tile(t, _):
            for i in range(3):
                out = [None] * (section * band // BLOCK)
                for b in range(section):
                    piece = arrived[source * section + b, :, pl.ds(pl.multiple_of(t * BLOCK, BLOCK), BLOCK)].astype(F32)
                    shift = (band * (b - i)) % BLOCK
                    if shift:
                        piece = pltpu.roll(piece, shift, 1)
                    at, begin = divmod(band * b, BLOCK)
                    if begin == 0:
                        out[at] = piece
                    else:
                        out[at] = jnp.where(lanes >= begin, piece, out[at])
                        if begin + band > BLOCK:
                            out[at + 1] = piece
                row = pl.multiple_of(t * 24 + i * 8, 8)
                for n, tile_value in enumerate(out):
                    regroup[pl.ds(row, 8), n * BLOCK : (n + 1) * BLOCK] = tile_value
            return 0

        lax.fori_loop(0, 4, tile, 0)
        gathered[q, h] = regroup[...].astype(BF16)
        for k, sem in ((1, left_recv), (3, right_recv)):
            pltpu.make_async_remote_copy(
                src_ref=gathered.at[q, h], dst_ref=gathered.at[q, h], send_sem=ring_send, recv_sem=sem.at[h],
                device_id=beside(0, other(k)), device_id_type=MESH,
            ).start()

    split = gathered.shape[2] // 2

    def forward(h):
        for origin, target, sem, far in ((3, 1, left_recv, 0), (1, 3, right_recv, 1)):
            whole = gathered.at[other(origin), h]
            pltpu.make_async_copy(whole, whole, sem.at[h]).wait()
            some = gathered.at[other(origin), h, pl.ds(far * split, split)]
            pltpu.make_async_remote_copy(
                src_ref=some, dst_ref=some, send_sem=ring_send, recv_sem=far_recv.at[far, h],
                device_id=beside(0, other(target)), device_id_type=MESH,
            ).start()

    wait_group(0)
    send_group(4)
    wait_group(1)
    send_group(5)
    regroup_chunk(0)
    wait_group(2)
    send_group(6)
    wait_group(3)
    send_group(7)
    regroup_chunk(1)
    forward(0)

    pltpu.make_async_copy(near, near, out_recv).wait()
    half_from[...] = near[:2].astype(BF16)
    for side in range(2):
        pltpu.make_async_remote_copy(
            src_ref=half_from, dst_ref=near_half.at[side], send_sem=half_send, recv_sem=half_recv,
            device_id=beside(1 - 2 * side, q), device_id_type=MESH,
        ).start()
    regroup_chunk(2)
    forward(1)
    regroup_chunk(3)
    for h in range(2):
        for c in range(tcols):
            cols = slice(c * BLOCK, (c + 1) * BLOCK)
            temp_out[h * 8 : (h + 1) * 8, cols] = near[h, c * 8 : (c + 1) * 8, :]
            salt_out[h * 8 : (h + 1) * 8, cols] = near[2 + h, c * 8 : (c + 1) * 8, :]

    columns = nlev * gathered.shape[2]
    each = columns // 4
    at = lax.broadcasted_iota(jnp.int32, (columns, 1), 0)
    s = sum((at >= n * each).astype(jnp.int32) for n in range(1, 4))
    rest = at - s * each
    lev_rows = 4 * levels
    from_q = sum((rest >= n * lev_rows).astype(jnp.int32) for n in range(1, nlev))
    rest = rest - from_q * lev_rows
    lev = rest // 4
    f, c = (rest // 2) % 2, rest % 2
    want = from_q * (16 * levels) + (f * levels + lev) * 8 + c * 4 + s
    perm = jnp.where(want == lax.broadcasted_iota(jnp.int32, (columns, columns), 1), 1.0, 0.0).astype(BF16)

    def contract(h):
        for far in range(2):
            some = gathered.at[other(2), h, pl.ds(far * split, split)]
            pltpu.make_async_copy(some, some, far_recv.at[far, h]).wait()
        whole = jnp.concatenate([gathered[k, h] for k in range(nlev)], axis=0)
        ordered = jnp.dot(perm, whole, preferred_element_type=F32).astype(BF16)
        source = lax.rem(high_at + 4 - h, 4)
        depth = section * band
        for s in range(4):
            term = jnp.dot(
                ordered[s * each : (s + 1) * each],
                leg[s, pl.ds(pl.multiple_of(source * depth, BLOCK), depth), :],
                preferred_element_type=F32,
            )
            spectra_ref[s] = term if h == 0 else spectra_ref[s] + term

    forward(2)
    leg_copy.wait()
    contract(0)
    forward(3)
    contract(1)

    pltpu.make_async_copy(near_half, near_half, half_recv).wait()
    mine = jnp.broadcast_to(slot_own[...].astype(F32), (BLOCK, per_lev)).T[:, :1]
    tiles = lax.broadcasted_iota(jnp.int32, (per_lev, part_rows), 1).astype(F32)
    surface = None
    for sec in range(3):
        for h in range(2):
            hot = jnp.where(mine == tiles + float((sec * 2 + h) * part_rows), 1.0, 0.0).astype(BF16)
            cells = near[h].astype(BF16) if sec == 1 else near_half[sec // 2, h]
            term = jnp.dot(hot, cells, preferred_element_type=F32)
            surface = term if surface is None else surface + term
    first_lane = lax.broadcasted_iota(jnp.int32, (band, BLOCK), 1)
    for b in range(lane_blocks):
        points = first_lane + (q * lane_blocks + b) * BLOCK
        base = (b // 3) * BLOCK + (b % 3) * band
        surface_ref[:, b * BLOCK : (b + 1) * BLOCK] = jnp.where(
            points < lat_col[:band, :], surface[base : base + band], 0.0
        )

    stores = [
        pltpu.make_async_copy(a, b, store_sem.at[n])
        for n, (a, b) in enumerate(
            ((temp_out, temp_to), (salt_out, salt_to), (surface_ref, surface_to), (spectra_ref, spectra_hbm))
        )
    ]
    for store in stores[:3]:
        store.start()
    contract(2)
    contract(3)
    stores[3].start()
    for store in stores:
        store.wait()

    for k in range(1, nlev):
        pltpu.make_async_copy(slot_own, slots.at[k], slot_send).wait()
    wait_group(4)
    wait_group(5)
    wait_group(6)
    wait_group(7)
    for k in range(3 * nlev - 1):
        pltpu.make_async_copy(parts.at[0, 0], sums.at[0, 0], part_send).wait()
    three = gathered.at[pl.ds(0, 3)]
    pltpu.make_async_copy(three, three, ring_send).wait()
    for k in range(1, nlev):
        pltpu.make_async_copy(fresh, near.at[0], out_send).wait()
    for side in range(2):
        pltpu.make_async_copy(half_from, near_half.at[0], half_send).wait()


def store_kernel(*refs):
    count = len(refs) // 2
    for n in range(count):
        refs[count + n][...] = refs[n][...]


def body(
    sizes,
    atmos_fields,
    lat_points,
    wave_order,
    legendre,
    column_weight,
    block_remap,
    ocean_temp,
    ocean_salt,
    sea_mask,
):
    nlat, nlev, nocn = sizes
    nf, nl, band, length = atmos_fields.shape
    groups = nlat * nocn
    rows = nf * nl * band
    waves = wave_order.shape[0]
    orow, ocols = ocean_temp.shape
    part_rows = orow * ocols // BLOCK // 2
    each, nj, degrees = legendre.shape
    depth = nj // 4
    quarter = length // nlev
    lanes = rows // (3 * band) * BLOCK
    per_lev = -(-(quarter // BLOCK) // 3) * BLOCK
    steps = length // CHUNK
    hbm = pl.BlockSpec(memory_space=pltpu.HBM)
    sem = pltpu.SemaphoreType.DMA
    outs = [
        jax.ShapeDtypeStruct((each, nlev * nl * nf * 2, degrees), F32),
        jax.ShapeDtypeStruct((orow, ocols), F32),
        jax.ShapeDtypeStruct((orow, ocols), F32),
        jax.ShapeDtypeStruct((band, quarter), F32),
    ]
    results = pl.pallas_call(
        functools.partial(fused_kernel, sizes),
        in_specs=[hbm] * 9,
        out_specs=[hbm] * 4,
        out_shape=outs,
        scratch_shapes=[pltpu.VMEM(o.shape, F32) for o in outs]
        + [
            sem((4,)),
            pltpu.SMEM((band,), jnp.int32),
            pltpu.VMEM((1, waves), jnp.int32),
            pltpu.VMEM(column_weight.shape, BF16),
            pltpu.VMEM(block_remap.shape[::-1], jnp.int32),
            pltpu.VMEM((steps, rows, CHUNK), BF16),
            pltpu.VMEM((orow, ocols), F32),
            pltpu.VMEM((orow, ocols), F32),
            pltpu.VMEM(sea_mask.shape, jnp.int32),
            pltpu.VMEM(legendre.shape, BF16),
            pltpu.VMEM((CHUNK, 2 * waves), BF16),
            pltpu.VMEM((CHUNK, 2 * waves), BF16),
            pltpu.VMEM((rows, 2 * waves), F32),
            pltpu.VMEM((lanes, 2 * waves), F32),
            pltpu.VMEM((nlev * per_lev, 2 * BLOCK), F32),
            pltpu.VMEM((nlev * per_lev, 4 * BLOCK), BF16),
            pltpu.VMEM((2, BLOCK, waves), F32),
            pltpu.VMEM((2, length // BLOCK, waves), F32),
            pltpu.VMEM((2 * band, BLOCK), jnp.int32),
            pltpu.VMEM((16, BLOCK), F32),
            pltpu.VMEM((1, per_lev), jnp.int32),
            pltpu.VMEM((groups, 2 * each, lanes), BF16),
            pltpu.VMEM((groups, 2 * each, lanes), BF16),
            pltpu.VMEM((nlev, 4, nl * nf * 8, depth), BF16),
            pltpu.VMEM((nl * nf * 8, depth), F32),
            pltpu.VMEM((3, nlev, part_rows, BLOCK), BF16),
            pltpu.VMEM((3, nlev, part_rows, BLOCK), BF16),
            pltpu.VMEM((nlev, 1, per_lev), jnp.int32),
            pltpu.VMEM((1, ocols), F32),
            pltpu.VMEM((1, ocols), F32),
            pltpu.VMEM((part_rows, BLOCK), F32),
            pltpu.VMEM((nlev, part_rows, BLOCK), F32),
            pltpu.VMEM((2, part_rows, BLOCK), BF16),
            pltpu.VMEM((2, 2, part_rows, BLOCK), BF16),
            sem((7,)), sem((steps,)), sem, sem((8,)), sem((4,)), sem, sem, sem, sem, sem, sem,
            sem, sem((4,)), sem((4,)), sem((2, 4)), sem, sem, sem, sem,
        ],
        compiler_params=pltpu.CompilerParams(
            collective_id=0, has_side_effects=True, vmem_limit_bytes=62 * 1024 * 1024
        ),
    )(
        lat_points, wave_order.reshape(1, waves), column_weight, block_remap.T, atmos_fields.reshape(rows, length),
        ocean_temp, ocean_salt, sea_mask, legendre,
    )
    return pl.pallas_call(store_kernel, out_shape=outs)(*results)


def solution(mesh):
    both = ("lat", "ocn")
    placed = (
        P(None, "lev", both, None),
        P(both),
        P(),
        P(both, None, "lev"),
        P(None, "lev"),
        P(both, "lev"),
        P(both, None),
        P(both, None),
        P(both, None),
    )
    sizes = tuple(mesh.shape[a] for a in ("lat", "lev", "ocn"))
    return jax.shard_map(
        functools.partial(body, sizes),
        mesh=mesh,
        in_specs=placed,
        out_specs=(P(both, None, "lev"), P(both, None), P(both, None), P(both, "lev")),
        check_vma=False,
    )
```
